512 devices in a mesh: pipe: 4 (over z_hi), dp: 16 (over y, x), tensor: 8 (over z_lo, core).
Axes of the slice: x: 4, y: 4, z: 16 (z_hi: 4, z_lo: 4; z = z_hi * 4 + z_lo), core: 2. Of those that a mesh axis runs over, the one named last changes fastest.
Arguments:
- x_in: bfloat16 [4, 2, 16, 128, 1600], P('pipe', None, 'dp', 'tensor'), may hold values from -6 to 6
- out_grad: bfloat16 [2, 16, 128, 1600], P(None, 'dp'), may hold values from -6 to 6
- layer_scale: float32 [4, 1600], P('pipe'), may hold values from 0.05 to 1
- norm_gain: float32 [4, 1600], P('pipe'), may hold values from 0.5 to 1.5
- master: float32 [4, 1600, 8192], P('pipe', 'dp', 'tensor'), may hold values from -0.15625 to 0.15625
- moment_one: float32 [4, 1600, 8192], P('pipe', 'dp', 'tensor'), may hold values from -4 to 4
- moment_two: float32 [4, 1600, 8192], P('pipe', 'dp', 'tensor'), may hold values from 0.05 to 5
Outputs:
- input_grads: bfloat16 [4, 2, 16, 128, 1600], P('pipe', None, 'dp', 'tensor')
- new_master: float32 [4, 1600, 8192], P('pipe', 'dp', 'tensor')
- new_moment_one: float32 [4, 1600, 8192], P('pipe', 'dp', 'tensor')
- new_moment_two: float32 [4, 1600, 8192], P('pipe', 'dp', 'tensor')
- scale_grads: float32 [4, 2, 1600], P('pipe')
The draws below stay inside these ranges and needn't reach their ends.
All inputs are finite; a program needn't handle non-finite values.
Results may differ from the reference program's by a relative error of at most 0.027.
Values may be sent and summed in bfloat16 or wider, within the bound.
A program may use at most 128 MiB of HBM per device.

```python
import math
import jax
import jax.numpy as jnp
from jax import lax

D = 1600
HEADS = 16
HD = 128
S = 128
MICRO = 2
IMAGES = 16
COLS = 8192
N_PIPE = 4
N_DP = 16
N_TENSOR = 8


def levels(own_key, shape, cuts, low, largest):
    def one(axis_at, parts):
        heights = jax.random.uniform(jax.random.fold_in(jax.random.fold_in(own_key, 6), axis_at), (parts,), jnp.float32, low / len(cuts), largest / len(cuts))
        return jnp.repeat(jnp.exp(heights), shape[axis_at] // parts).reshape((-1,) + (1,) * (len(shape) - axis_at - 1))

    factor_of = one(*cuts[0])
    for cut in cuts[1:]:
        factor_of = factor_of * one(*cut)
    return factor_of


def scatter_about(rng, extent, deviation, bound, cuts=(), dtype=jnp.bfloat16):
    drawn = jax.random.normal(rng, extent, jnp.float32) * deviation
    if len(cuts) > 0:
        drawn = levels(rng, extent, cuts, -0.22, 0.18) * drawn
    return jnp.clip(drawn, min=-bound, max=bound).astype(dtype)


def setup_inputs(seed: int = 0) -> dict:
    key_list = jax.random.split(jax.random.key(seed), 8)
    x_in = scatter_about(key_list[0], (N_PIPE, MICRO, IMAGES, S, D), 1.0, 6.0, ((0, 4), (2, 16), (3, 8)))
    out_grad = scatter_about(key_list[1], (MICRO, IMAGES, S, D), 1.0, 6.0, ((1, 16),))
    layer_scale = jnp.clip(jnp.exp(math.log(1.0) - 2.9957323 * jax.random.uniform(key_list[2], (N_PIPE, D), jnp.float32) ** levels(key_list[2], (N_PIPE, D), ((0, 4),), -0.2, 0.2)), 0.05, 1.0)
    norm_gain = jnp.clip(1.0 + 0.1 * jax.random.normal(key_list[3], (N_PIPE, D), jnp.float32), 0.5, 1.5)
    master = scatter_about(key_list[4], (N_PIPE, D, COLS), D ** -0.5, 0.15625, ((0, 4), (1, 16), (2, 8)), jnp.float32)
    moment_one = scatter_about(key_list[5], (N_PIPE, D, COLS), 0.3, 4.0, ((0, 4), (1, 16), (2, 8)), jnp.float32)
    moment_two = jnp.clip(jnp.exp(math.log(5.0) - 4.6051702 * jax.random.uniform(key_list[6], (N_PIPE, D, COLS), jnp.float32) ** levels(key_list[6], (N_PIPE, D, COLS), ((0, 4), (1, 16), (2, 8)), -0.2, 0.2)), 0.05, 5.0)
    return {"x_in": x_in, "out_grad": out_grad, "layer_scale": layer_scale, "norm_gain": norm_gain, "master": master, "moment_one": moment_one, "moment_two": moment_two}


beta_one = 0.9
beta_two = 0.95
adam_eps = 1e-08
learn_rate = 0.001
weight_decay = 0.05
adam_step = 100.0
norm_eps = 1e-06

def split_columns(weights):
    row_count = weights.shape[0]
    groups = weights.reshape(row_count, N_TENSOR, 4, weights.shape[1] // (4 * N_TENSOR))
    return [groups[:, :, member].reshape(row_count, -1) for member in range(4)]

def join_columns(members):
    row_count = members[0].shape[0]
    stacked = jnp.stack([member.reshape(row_count, N_TENSOR, -1) for member in members], axis=2)
    return stacked.reshape(row_count, -1)

def by_replica(array):
    shape = array.shape
    split = array.reshape(shape[:1] + (N_DP, shape[1] // N_DP) + shape[2:])
    return jnp.moveaxis(split, 1, 0)

def product(form, left, right):
    return jnp.einsum(form, left.astype(jnp.float32), right.astype(jnp.float32))

def rounded(value):
    return lax.optimization_barrier(value.astype(jnp.bfloat16)).astype(jnp.float32)

def reference(x_in, out_grad, layer_scale, norm_gain, master, moment_one, moment_two):
    score_root = math.sqrt(HD)
    group_width = HEADS * HD // N_TENSOR
    bias_one = 1.0 - beta_one ** adam_step
    bias_two = 1.0 - beta_two ** adam_step
    incoming = out_grad
    passed_list = [None] * N_PIPE
    master_list = [None] * N_PIPE
    first_list = [None] * N_PIPE
    second_list = [None] * N_PIPE
    scale_list = [None] * N_PIPE
    for section in range(N_PIPE - 1, -1, -1):
        weights = master[section].astype(jnp.bfloat16)
        w_query, w_keys, w_values, w_out = split_columns(weights)
        gain_vec = norm_gain[section]
        scale_vec = layer_scale[section]
        activations = x_in[section].astype(jnp.float32)
        inverse = lax.rsqrt(lax.optimization_barrier(jnp.mean(activations * activations, axis=-1, keepdims=True)) + norm_eps)
        unit_rows = activations * inverse
        normed = (unit_rows * gain_vec).astype(jnp.bfloat16)
        query = product('mbsd,dc->mbsc', normed, w_query).astype(jnp.bfloat16)
        keys = product('mbsd,dc->mbsc', normed, w_keys).astype(jnp.bfloat16)
        values = product('mbsd,dc->mbsc', normed, w_values).astype(jnp.bfloat16)
        heads_shape = query.shape[:3] + (HEADS, HD)
        query_heads = query.reshape(heads_shape)
        keys_heads = keys.reshape(heads_shape)
        values_heads = values.reshape(heads_shape)
        probs = jax.nn.softmax(product('mbqhe,mbkhe->mbhqk', query_heads, keys_heads) / score_root, axis=-1)
        probs_low = probs.astype(jnp.bfloat16)
        attended = product('mbhqk,mbkhe->mbqhe', probs_low, values_heads).astype(jnp.bfloat16)
        attended_flat = attended.reshape(query.shape)
        grad_wide = incoming.astype(jnp.float32)
        scaled = (scale_vec * grad_wide).astype(jnp.bfloat16)
        d_att = product('mbsd,dc->mbsc', scaled, w_out).astype(jnp.bfloat16)
        d_att_heads = d_att.reshape(heads_shape)
        d_prob = product('mbqhe,mbkhe->mbhqk', d_att_heads, values_heads)
        row_delta = product('mbqhe,mbqhe->mbhq', d_att_heads, attended)
        d_score = (probs * (d_prob - row_delta[..., None]) / score_root).astype(jnp.bfloat16)
        d_query = product('mbhqk,mbkhe->mbqhe', d_score, keys_heads).astype(jnp.bfloat16).reshape(query.shape)
        d_keys = product('mbhqk,mbqhe->mbkhe', d_score, query_heads).astype(jnp.bfloat16).reshape(query.shape)
        d_values = product('mbhqk,mbqhe->mbkhe', probs_low, d_att_heads).astype(jnp.bfloat16).reshape(query.shape)
        d_normed = jnp.zeros(activations.shape, jnp.float32)
        for tensor_group in range(N_TENSOR):
            col_start = tensor_group * group_width
            col_end = col_start + group_width
            group_sum = product('mbsc,dc->mbsd', d_query[..., col_start:col_end], w_query[:, col_start:col_end])
            group_sum = group_sum + product('mbsc,dc->mbsd', d_keys[..., col_start:col_end], w_keys[:, col_start:col_end])
            group_sum = group_sum + product('mbsc,dc->mbsd', d_values[..., col_start:col_end], w_values[:, col_start:col_end])
            d_normed = d_normed + rounded(group_sum)
        d_unit = d_normed * gain_vec
        d_input = inverse * (d_unit - unit_rows * lax.optimization_barrier(jnp.mean(d_unit * unit_rows, axis=-1, keepdims=True)))
        passed = (grad_wide + d_input).astype(jnp.bfloat16)
        output_proj = product('mbsc,dc->mbsd', attended_flat, w_out)
        scale_grad = lax.optimization_barrier(jnp.sum(grad_wide * output_proj, axis=(0, 1, 2)))
        gain_grad = lax.optimization_barrier(jnp.sum(d_normed * unit_rows, axis=(0, 1, 2)))

        def replica_sum(total, pieces):
            p_normed, p_query, p_keys, p_values, p_scaled, p_attended = pieces
            members = [product('mbsd,mbsc->dc', p_normed, p_query), product('mbsd,mbsc->dc', p_normed, p_keys), product('mbsd,mbsc->dc', p_normed, p_values), product('mbsd,mbsc->dc', p_scaled, p_attended)]
            return (total + rounded(join_columns(members)), None)
        stacked_inputs = tuple((by_replica(array) for array in (normed, d_query, d_keys, d_values, scaled, attended_flat)))
        weight_grad = lax.scan(replica_sum, jnp.zeros(master.shape[1:], jnp.float32), stacked_inputs)[0]
        first_new = beta_one * moment_one[section] + (1.0 - beta_one) * weight_grad
        second_new = beta_two * moment_two[section] + (1.0 - beta_two) * weight_grad * weight_grad
        update = first_new / bias_one / (jnp.sqrt(second_new / bias_two) + adam_eps)
        master_new = master[section] - learn_rate * (update + weight_decay * master[section])
        passed_list[section] = passed
        master_list[section] = master_new
        first_list[section] = first_new
        second_list[section] = second_new
        scale_list[section] = jnp.stack([scale_grad, gain_grad])
        incoming = passed
    return (jnp.stack(passed_list), jnp.stack(master_list), jnp.stack(first_list), jnp.stack(second_list), jnp.stack(scale_list))
```

```python
import math

import jax
import jax.numpy as jnp
from jax import lax
from jax.sharding import PartitionSpec as P

HD = 128


beta_one = 0.9
beta_two = 0.95
adam_eps = 1e-08
learn_rate = 0.001
weight_decay = 0.05
adam_step = 100.0
norm_eps = 1e-06


def from_behind(block, axis, distance):
    devices = range(lax.axis_size(axis))
    route = [(i - distance, i) for i in devices if i - distance in devices]
    return lax.ppermute(block, axis, route)


def normalize(values_in):
    inverse = lax.rsqrt(jnp.mean(values_in * values_in, axis=-1, keepdims=True) + norm_eps)
    return (inverse, values_in * inverse)


def select_micro(array, micro_index):
    return lax.dynamic_index_in_dim(array, micro_index, 0, keepdims=False)


def store_slot(buffer, value, slot_index):
    return lax.dynamic_update_index_in_dim(buffer, value, slot_index, 0)


def local(x_in, out_grad, layer_scale, norm_gain, master, moment_one, moment_two):
    n_pipe = lax.axis_size("pipe")
    n_tensor = lax.axis_size("tensor")
    pipe_rank = lax.axis_index("pipe")
    micro_count = x_in.shape[1]
    images = x_in.shape[2]
    shard_len = x_in.shape[3]
    channels = x_in.shape[4]
    seq_len = shard_len * n_tensor
    row_start = lax.axis_index("tensor") * shard_len
    head_cols = master.shape[2] // 4
    local_heads = head_cols // HD
    score_root = math.sqrt(HD)
    scale_vec = layer_scale[0]
    gain_vec = norm_gain[0]
    weights = lax.all_gather(master[0].astype(jnp.bfloat16), "dp", axis=0, tiled=True)
    w_qkv = weights[:, : 3 * head_cols]
    w_out = weights[:, 3 * head_cols :]
    full_x = lax.all_gather(x_in[0], "tensor", axis=2, tiled=True).astype(jnp.float32)
    full_inverse, full_unit = normalize(full_x)
    normed = (full_unit * gain_vec).astype(jnp.bfloat16)
    local_unit = lax.dynamic_slice_in_dim(full_unit, row_start, shard_len, 2)
    local_inverse = lax.dynamic_slice_in_dim(full_inverse, row_start, shard_len, 2)
    projected = jnp.einsum(
        "mbsd,dc->mbsc", normed, w_qkv, preferred_element_type=jnp.float32
    ).astype(jnp.bfloat16)
    projected = projected.reshape(micro_count, images, seq_len, 3, local_heads, HD)
    query = projected[:, :, :, 0]
    keys = projected[:, :, :, 1]
    values = projected[:, :, :, 2]
    scores = (
        jnp.einsum("mbqhe,mbkhe->mbhqk", query, keys, preferred_element_type=jnp.float32)
        / score_root
    )
    probs = jax.nn.softmax(scores, axis=-1)
    probs_low = probs.astype(jnp.bfloat16)
    attended = jnp.einsum(
        "mbhqk,mbkhe->mbqhe", probs_low, values, preferred_element_type=jnp.float32
    ).astype(jnp.bfloat16)
    attended_flat = attended.reshape(micro_count, images, seq_len, head_cols)

    def backward_segment(micro_index, incoming):
        query_now = select_micro(query, micro_index)
        keys_now = select_micro(keys, micro_index)
        values_now = select_micro(values, micro_index)
        probs_now = select_micro(probs, micro_index)
        probs_low_now = select_micro(probs_low, micro_index)
        attended_now = select_micro(attended, micro_index)
        scaled = (scale_vec * incoming.astype(jnp.float32)).astype(jnp.bfloat16)
        d_att = jnp.einsum("bsd,dc->bsc", scaled, w_out, preferred_element_type=jnp.float32).astype(
            jnp.bfloat16
        )
        d_att = d_att.reshape(images, seq_len, local_heads, HD)
        d_prob = jnp.einsum(
            "bqhe,bkhe->bhqk", d_att, values_now, preferred_element_type=jnp.float32
        )
        row_delta = jnp.einsum(
            "bqhe,bqhe->bhq", d_att, attended_now, preferred_element_type=jnp.float32
        )
        d_score = (probs_now * (d_prob - row_delta[..., None]) / score_root).astype(jnp.bfloat16)
        d_query = jnp.einsum(
            "bhqk,bkhe->bqhe", d_score, keys_now, preferred_element_type=jnp.float32
        ).astype(jnp.bfloat16)
        d_keys = jnp.einsum(
            "bhqk,bqhe->bkhe", d_score, query_now, preferred_element_type=jnp.float32
        ).astype(jnp.bfloat16)
        d_values = jnp.einsum(
            "bhqk,bqhe->bkhe", probs_low_now, d_att, preferred_element_type=jnp.float32
        ).astype(jnp.bfloat16)
        d_proj = jnp.concatenate([d_query, d_keys, d_values], axis=2).reshape(
            images, seq_len, 3 * head_cols
        )
        partial_sum = jnp.einsum("bsc,dc->bsd", d_proj, w_qkv, preferred_element_type=jnp.float32)
        return (partial_sum, d_proj, scaled)

    def spare_segment(micro_index, incoming):
        return (
            jnp.zeros((images, seq_len, channels), jnp.float32),
            jnp.zeros((images, seq_len, 3 * head_cols), jnp.bfloat16),
            jnp.zeros((images, seq_len, channels), jnp.bfloat16),
        )

    segments = n_pipe + micro_count - 1
    is_last = pipe_rank == n_pipe - 1
    received = jnp.zeros((images, seq_len, channels), jnp.bfloat16)
    slots = micro_count + 1
    grads_out = jnp.zeros((slots, images, shard_len, channels), jnp.bfloat16)
    proj_saved = jnp.zeros((slots, images, seq_len, 3 * head_cols), jnp.bfloat16)
    scaled_saved = jnp.zeros((slots, images, seq_len, channels), jnp.bfloat16)
    grad_saved = jnp.zeros((slots, images, seq_len, channels), jnp.bfloat16)
    gain_part = jnp.zeros((channels,), jnp.float32)
    for segment_step in range(segments):
        micro_index = segment_step - (n_pipe - 1) + pipe_rank
        active = jnp.logical_and(micro_index >= 0, micro_index < micro_count)
        micro_index = jnp.clip(micro_index, 0, micro_count - 1)
        slot_index = jnp.where(active, micro_index, micro_count)
        arrived = received
        incoming = jnp.where(is_last, select_micro(out_grad, micro_index), arrived)
        partial_sum, d_proj, scaled = lax.cond(
            active, backward_segment, spare_segment, micro_index, incoming
        )
        pieces = partial_sum.astype(jnp.bfloat16).reshape(images, n_tensor, shard_len, channels)
        landed = lax.all_to_all(pieces, "tensor", split_axis=1, concat_axis=1, tiled=True)
        own_d = jnp.sum(landed.astype(jnp.float32), axis=1)
        own_unit = select_micro(local_unit, micro_index)
        own_inverse = select_micro(local_inverse, micro_index)
        d_unit = own_d * gain_vec
        d_input = own_inverse * (
            d_unit - own_unit * jnp.mean(d_unit * own_unit, axis=-1, keepdims=True)
        )
        own_incoming = lax.dynamic_slice_in_dim(incoming, row_start, shard_len, 1)
        own_passed = (own_incoming.astype(jnp.float32) + d_input).astype(jnp.bfloat16)
        gain_part = gain_part + jnp.where(active, jnp.sum(own_d * own_unit, axis=(0, 1)), 0.0)
        grads_out = store_slot(grads_out, own_passed, slot_index)
        proj_saved = store_slot(proj_saved, d_proj, slot_index)
        scaled_saved = store_slot(scaled_saved, scaled, slot_index)
        grad_saved = store_slot(grad_saved, incoming, slot_index)
        if segment_step + 1 < segments:
            moved = from_behind(own_passed, "pipe", -1)
            received = lax.all_gather(moved, "tensor", axis=1, tiled=True)
    grads_kept = grads_out[:micro_count]
    proj_kept = proj_saved[:micro_count]
    scaled_kept = scaled_saved[:micro_count]
    grad_kept = grad_saved[:micro_count]
    grad_qkv = jnp.einsum("mbsd,mbsc->dc", normed, proj_kept, preferred_element_type=jnp.float32)
    grad_out = jnp.einsum(
        "mbsd,mbsc->dc", scaled_kept, attended_flat, preferred_element_type=jnp.float32
    )
    weight_grad = lax.psum_scatter(
        jnp.concatenate([grad_qkv, grad_out], axis=1).astype(jnp.bfloat16),
        "dp",
        scatter_dimension=0,
        tiled=True,
    ).astype(jnp.float32)
    summed_out = jnp.einsum(
        "mbsd,mbsc->dc", grad_kept, attended_flat, preferred_element_type=jnp.float32
    )
    scale_part = jnp.sum(w_out.astype(jnp.float32) * summed_out, axis=1)
    scale_both = lax.psum(lax.psum(jnp.stack([scale_part, gain_part]), "tensor"), "dp")
    bias_one = 1.0 - beta_one**adam_step
    bias_two = 1.0 - beta_two**adam_step
    first_new = beta_one * moment_one[0] + (1.0 - beta_one) * weight_grad
    second_new = beta_two * moment_two[0] + (1.0 - beta_two) * weight_grad * weight_grad
    update = first_new / bias_one / (jnp.sqrt(second_new / bias_two) + adam_eps)
    master_new = master[0] - learn_rate * (update + weight_decay * master[0])
    return (grads_kept[None], master_new[None], first_new[None], second_new[None], scale_both[None])


def solution(mesh):
    placed = (
        P("pipe", None, "dp", "tensor", None),
        P(None, "dp", None, None),
        P("pipe", None),
        P("pipe", None),
        P("pipe", "dp", "tensor"),
        P("pipe", "dp", "tensor"),
        P("pipe", "dp", "tensor"),
    )
    return jax.shard_map(
        local,
        mesh=mesh,
        in_specs=placed,
        out_specs=(
            P("pipe", None, "dp", "tensor", None),
            P("pipe", "dp", "tensor"),
            P("pipe", "dp", "tensor"),
            P("pipe", "dp", "tensor"),
            P("pipe", None, None),
        ),
        check_vma=False,
    )
```

```python
import functools
import math

import jax
import jax.numpy as jnp
from jax import lax
from jax.experimental import pallas as pl
from jax.experimental.pallas import tpu as pltpu
from jax.sharding import PartitionSpec as P

HD = 128
D = 1600
ROWS = 100
WIDE = 256
SIDE = 4

beta_one = 0.9
beta_two = 0.95
adam_eps = 1e-08
learn_rate = 0.001
weight_decay = 0.05
adam_step = 100.0
norm_eps = 1e-06

F32 = jnp.float32
BF16 = jnp.bfloat16
MESH = pl.DeviceIdType.MESH


def dot(left, right, dims):
    return lax.dot_general(left, right, ((dims[:1], dims[1:]), ((), ())), preferred_element_type=F32)


def kernel(
    x_ref, og_ref, ls_ref, gain_ref, master_ref, one_ref, two_ref,
    ig_ref, nm_ref, n1_ref, n2_ref, sg_ref,
    wland, dense, wide, xall, normed, qkv, probs, att, outproj, inc, scaled, dproj,
    part, s1land, pair, s2land, own_out, gsend, gland1, gmid, gmid_send, gland2, small, sm_t, sm_d, sm_send,
    w_ss, w_rs, x_ss, x_rs, a_ss, a_rs, c_ss, c_rs, g_ss, g_rs, t_ss, t_rs, d_ss, d_rs,
):
    p = lax.axis_index("pipe")
    r = lax.axis_index("dp")
    t = lax.axis_index("tensor")
    chip = t // 2
    core = t % 2
    y = r // SIDE
    x = r % SIDE
    partner = chip * 2 + (1 - core)
    root = math.sqrt(HD)

    def up(v, by):
        return lax.rem(v + by, SIDE)

    def send(src, dst, ss, rs, where):
        copy = pltpu.make_async_remote_copy(
            src_ref=src, dst_ref=dst, send_sem=ss, recv_sem=rs, device_id=where, device_id_type=MESH
        )
        copy.start()
        return copy

    def landed(dst, rs):
        pltpu.make_async_remote_copy(
            src_ref=dst, dst_ref=dst, send_sem=rs, recv_sem=rs,
            device_id={"tensor": partner}, device_id_type=MESH,
        ).wait_recv()

    for q in range(4):
        wland[q, r] = master_ref[:, q * WIDE : (q + 1) * WIDE].astype(BF16)

    barrier = pltpu.get_barrier_semaphore()
    for k in range(1, 16):
        pl.semaphore_signal(barrier, inc=1, device_id={"dp": lax.rem(r + k, 16)}, device_id_type=MESH)
    for k in range(1, 8):
        pl.semaphore_signal(barrier, inc=1, device_id={"tensor": lax.rem(t + k, 8)}, device_id_type=MESH)
    for k in (1, 3):
        pl.semaphore_signal(barrier, inc=1, device_id={"pipe": lax.rem(p + k, 4)}, device_id_type=MESH)
    pl.semaphore_wait(barrier, 24)

    def at(h, near, far):
        return far * SIDE + near if h == 0 else near * SIDE + far

    def coords(h):
        return (x, y) if h == 0 else (y, x)

    def spread(buf, ss, rs):
        copies = [send(buf.at[t], buf.at[t], ss.at[0], rs.at[t], {"tensor": partner})]
        for k in range(1, 4):
            other = up(chip, k) * 2 + core
            copies.append(send(buf.at[t], buf.at[t], ss.at[k], rs.at[t], {"tensor": other}))
        return copies

    def relay(buf, ss, rs):
        copies = []
        for k in range(1, 4):
            other = up(chip, k) * 2 + core
            landed(buf.at[other], rs.at[other])
            copies.append(send(buf.at[other], buf.at[other], ss.at[3 + k], rs.at[other], {"tensor": partner}))
        return copies

    def settle(buf, rs):
        landed(buf.at[partner], rs.at[partner])
        for k in range(1, 4):
            other = up(chip, k) * 2 + 1 - core
            landed(buf.at[other], rs.at[other])

    pending = []

    def wsend(q, s, slot, where):
        pending.append(send(wland.at[q, s], wland.at[q, s], w_ss.at[q, slot], w_rs.at[q, s], {"dp": where}))

    for h in range(2):
        near, far = coords(h)
        for q in (2 * h, 2 * h + 1):
            wsend(q, r, 0, at(h, up(near, 1), far))
            wsend(q, r, 1, at(h, up(near, 3), far))
    xall[t] = x_ref[...]
    x_copies = spread(xall, x_ss, x_rs)
    for h in range(2):
        near, far = coords(h)
        for q in (2 * h, 2 * h + 1):
            wsend(q, r, 3, at(h, near, up(far, 1)))
            wsend(q, r, 4, at(h, near, up(far, 3)))
    for h in range(2):
        near, far = coords(h)
        for q in (2 * h, 2 * h + 1):
            below = at(h, up(near, 3), far)
            above = at(h, up(near, 1), far)
            landed(wland.at[q, below], w_rs.at[q, below])
            if q % 2 == 0:
                wsend(q, below, 2, above)
            landed(wland.at[q, above], w_rs.at[q, above])
            if q % 2 == 1:
                wsend(q, above, 2, below)
            for j, s in ((1, below), (2, above)):
                wsend(q, s, 3 + 3 * j, at(h, near, up(far, 1)))
                wsend(q, s, 4 + 3 * j, at(h, near, up(far, 3)))
    for h in range(2):
        near, far = coords(h)
        for q in (2 * h, 2 * h + 1):
            s = at(h, up(near, 2), far)
            landed(wland.at[q, s], w_rs.at[q, s])
            wsend(q, s, 12, at(h, near, up(far, 1)))
            wsend(q, s, 13, at(h, near, up(far, 3)))
    x_copies += relay(xall, x_ss, x_rs)
    settle(xall, x_rs)

    gain = gain_ref[...]
    for m in range(2):
        rows = xall[:, m].reshape(128, D).astype(F32)
        inverse = lax.rsqrt(jnp.mean(rows * rows, axis=-1, keepdims=True) + norm_eps)
        normed[m * 128 : (m + 1) * 128] = (rows * inverse * gain).astype(BF16)

    @pl.when(p == 3)
    def _():
        inc[...] = og_ref[...]

    for j, step in enumerate((0, 3, 1, 2)):
        for h in range(2):
            near, far = coords(h)
            for q in (2 * h, 2 * h + 1):
                lower = at(h, up(near, step), up(far, 3))
                upper = at(h, up(near, step), up(far, 1))
                landed(wland.at[q, lower], w_rs.at[q, lower])
                if q % 2 == 0:
                    wsend(q, lower, 5 + 3 * j, at(h, near, up(far, 1)))
                landed(wland.at[q, upper], w_rs.at[q, upper])
                if q % 2 == 1:
                    wsend(q, upper, 5 + 3 * j, at(h, near, up(far, 3)))
    for h in range(2):
        near, far = coords(h)
        for q in (2 * h, 2 * h + 1):
            for step in range(4):
                s = at(h, up(near, step), up(far, 2))
                landed(wland.at[q, s], w_rs.at[q, s])

    for q in range(4):
        for s in range(16):
            wide[s * ROWS : (s + 1) * ROWS] = wland[q, s].astype(F32)
        dense[q] = wide[...].astype(BF16)
        if q < 3:
            qkv[q] = dot(normed[...], dense[q], (1, 0)).astype(BF16)
    for m in range(2):
        row = slice(m * 128, (m + 1) * 128)
        for head in range(2):
            col = slice(head * HD, (head + 1) * HD)
            scores = dot(qkv[0, row, col], qkv[1, row, col], (1, 1)) / root
            scores = jnp.exp(scores - jnp.max(scores, axis=-1, keepdims=True))
            prob = scores / jnp.sum(scores, axis=-1, keepdims=True)
            probs[m, head] = prob
            att[row, col] = dot(prob.astype(BF16), qkv[2, row, col], (1, 0)).astype(BF16)

    def backward(m):
        row = slice(m * 128, (m + 1) * 128)
        scaled_now = (ls_ref[...] * inc[m].reshape(128, D).astype(F32)).astype(BF16)
        scaled[row] = scaled_now
        d_att = dot(scaled_now, dense[3], (1, 0)).astype(BF16)
        for head in range(2):
            col = slice(head * HD, (head + 1) * HD)
            d_now = d_att[:, col]
            d_prob = dot(d_now, qkv[2, row, col], (1, 1))
            delta = jnp.sum(d_now.astype(F32) * att[row, col].astype(F32), axis=-1, keepdims=True)
            prob = probs[m, head]
            d_score = (prob * (d_prob - delta) / root).astype(BF16)
            dproj[0, row, col] = dot(d_score, qkv[1, row, col], (1, 0)).astype(BF16)
            dproj[1, row, col] = dot(d_score, qkv[0, row, col], (0, 0)).astype(BF16)
            dproj[2, row, col] = dot(prob.astype(BF16), d_now, (0, 0)).astype(BF16)
        total = dot(dproj[0, row], dense[0], (1, 1))
        total += dot(dproj[1, row], dense[1], (1, 1))
        total += dot(dproj[2, row], dense[2], (1, 1))
        total = total.astype(BF16)
        for other in range(8):
            part[m, other % 2, other // 2] = total[other * 16 : (other + 1) * 16]

    def scale_part(m):
        row = slice(m * 128, (m + 1) * 128)
        out_rows = dot(att[row], dense[3], (1, 1))
        return jnp.sum(inc[m].reshape(128, D).astype(F32) * out_rows, axis=0, keepdims=True)

    def first_stage(m):
        return [
            send(part.at[m, 1 - core], s1land.at[m], c_ss.at[m, 0], c_rs.at[m, 0], {"tensor": partner})
        ]

    def second_stage(m):
        landed(s1land.at[m], c_rs.at[m, 0])
        pair[m] = (part[m, core].astype(F32) + s1land[m].astype(F32)).astype(BF16)
        copies = []
        for k in range(1, 4):
            to = up(chip, k)
            copies.append(
                send(pair.at[m, to], s2land.at[m, chip], c_ss.at[m, k], c_rs.at[m, 1 + chip], {"tensor": to * 2 + core})
            )
        return copies

    def finish(m):
        total = pair[m, chip].astype(F32)
        for k in range(1, 4):
            other = up(chip, k)
            landed(s2land.at[m, other], c_rs.at[m, 1 + other])
            total += s2land[m, other].astype(F32)
        rows = x_ref[m].astype(F32)
        inverse = lax.rsqrt(jnp.mean(rows * rows, axis=-1, keepdims=True) + norm_eps)
        unit = rows * inverse
        e = total * gain
        d_input = inverse * (e - unit * jnp.mean(e * unit, axis=-1, keepdims=True))
        passed = (inc[m, t].astype(F32) + d_input).astype(BF16)
        own_out[m] = passed
        ig_ref[m] = passed
        return jnp.sum(total * unit, axis=0, keepdims=True)

    def hand_on(m):
        return pltpu.make_async_remote_copy(
            src_ref=own_out.at[m], dst_ref=inc.at[m, t], send_sem=c_ss.at[m, 4], recv_sem=a_rs.at[m, t],
            device_id={"pipe": lax.rem(p + 3, 4)}, device_id_type=MESH,
        )

    def take_in(m):
        @pl.when(p < 3)
        def _():
            landed(inc.at[m, t], a_rs.at[m, t])
            copies = spread(inc.at[m], a_ss.at[m], a_rs.at[m])
            copies += relay(inc.at[m], a_ss.at[m], a_rs.at[m])
            settle(inc.at[m], a_rs.at[m])
            for copy in copies:
                copy.wait_send()

    scale_sum = jnp.zeros((1, D), F32)
    gain_sum = jnp.zeros((1, D), F32)
    for m in range(2):
        take_in(m)
        backward(m)
        pending += first_stage(m)
        pending += second_stage(m)
        scale_sum += scale_part(m)
        gain_sum += finish(m)

        @pl.when(p > 0)
        def _():
            hand_on(m).start()

    small[0:1] = scale_sum
    small[1:2] = gain_sum
    for k in range(1, 8):
        other = lax.rem(t + k, 8)
        pending.append(send(small, sm_t.at[t], t_ss.at[k], t_rs.at[t], {"tensor": other}))

    for copy in pending[:60]:
        copy.wait_send()
    pending = pending[60:]
    for q in (3, 0, 1, 2):
        h = q // 2
        if q == 3:
            wide[...] = dot(scaled[...], att[...], (0, 0))
        else:
            wide[...] = dot(normed[...], dproj[q], (0, 0))
        for s in range(16):
            place = s if h == 0 else (s % SIDE) * SIDE + s // SIDE
            gsend[q, place // SIDE, place % SIDE] = wide[s * ROWS : (s + 1) * ROWS].astype(BF16)

    def gcopy(q, kind, src, where, second):
        h = q // 2
        near, far = coords(h)
        if second:
            to = at(h, up(near, where), far)
            slot, land = 3 + kind, gland2.at[q, kind]
        else:
            to = at(h, near, up(far, where))
            slot, land = kind, gland1.at[q, kind]
        pending.append(send(src, land, g_ss.at[q, slot], g_rs.at[q, slot], {"dp": to}))

    order = (3, 0, 1, 2)
    for q in order:
        near, far = coords(q // 2)
        ahead, back = (1, 3) if q % 2 == 0 else (3, 1)
        gcopy(q, 0, gsend.at[q, up(far, 2)], ahead, False)
        gcopy(q, 1, gsend.at[q, up(far, back)], back, False)
    for q in order:
        near, far = coords(q // 2)
        ahead, back = (1, 3) if q % 2 == 0 else (3, 1)
        landed(gland1.at[q, 0], g_rs.at[q, 0])
        line = up(far, ahead)
        gsend[q, line] = (gsend[q, line].astype(F32) + gland1[q, 0].astype(F32)).astype(BF16)
        gcopy(q, 2, gsend.at[q, line], ahead, False)

    total = small[...]
    for k in range(1, 8):
        other = lax.rem(t + k, 8)
        landed(sm_t.at[other], t_rs.at[other])
        total += sm_t[other]
    sm_send[...] = total
    for k in range(1, 16):
        other = lax.rem(r + k, 16)
        pending.append(send(sm_send, sm_d.at[r], d_ss.at[k], d_rs.at[r], {"dp": other}))

    for q in order:
        near, far = coords(q // 2)
        ahead, back = (1, 3) if q % 2 == 0 else (3, 1)
        landed(gland1.at[q, 1], g_rs.at[q, 1])
        landed(gland1.at[q, 2], g_rs.at[q, 2])
        gmid[q] = gsend[q, far].astype(F32) + gland1[q, 1].astype(F32) + gland1[q, 2].astype(F32)
        gmid_send[q] = gmid[q].astype(BF16)
        gcopy(q, 0, gmid_send.at[q, up(near, 2)], ahead, True)
        gcopy(q, 1, gmid_send.at[q, up(near, back)], back, True)
    for q in order:
        near, far = coords(q // 2)
        ahead, back = (1, 3) if q % 2 == 0 else (3, 1)
        landed(gland2.at[q, 0], g_rs.at[q, 3])
        line = up(near, ahead)
        gmid_send[q, line] = (gmid[q, line] + gland2[q, 0].astype(F32)).astype(BF16)
        gcopy(q, 2, gmid_send.at[q, line], ahead, True)

    bias_one = 1.0 - beta_one**adam_step
    bias_two = 1.0 - beta_two**adam_step
    for q in order:
        near, far = coords(q // 2)
        landed(gland2.at[q, 1], g_rs.at[q, 4])
        landed(gland2.at[q, 2], g_rs.at[q, 5])
        grad = gmid[q, near] + gland2[q, 1].astype(F32) + gland2[q, 2].astype(F32)
        cols = slice(q * WIDE, (q + 1) * WIDE)
        first = beta_one * one_ref[:, cols] + (1.0 - beta_one) * grad
        second = beta_two * two_ref[:, cols] + (1.0 - beta_two) * grad * grad
        update = first / bias_one / (jnp.sqrt(second / bias_two) + adam_eps)
        old = master_ref[:, cols]
        nm_ref[:, cols] = old - learn_rate * (update + weight_decay * old)
        n1_ref[:, cols] = first
        n2_ref[:, cols] = second

    total = sm_send[...]
    for k in range(1, 16):
        other = lax.rem(r + k, 16)
        landed(sm_d.at[other], d_rs.at[other])
        total += sm_d[other]
    sg_ref[...] = total

    for copy in pending + x_copies:
        copy.wait_send()

    @pl.when(p > 0)
    def _():
        for m in range(2):
            hand_on(m).wait_send()


def local(x_in, out_grad, layer_scale, norm_gain, master, moment_one, moment_two):
    vmem = pl.BlockSpec(memory_space=pltpu.VMEM)
    shard = jax.ShapeDtypeStruct((ROWS, 4 * WIDE), F32)
    dma = pltpu.SemaphoreType.DMA
    scratch = [
        pltpu.VMEM((4, 16, ROWS, WIDE), BF16),
        pltpu.VMEM((4, D, WIDE), BF16),
        pltpu.VMEM((D, WIDE), F32),
        pltpu.VMEM((8, 2, 16, D), BF16),
        pltpu.VMEM((256, D), BF16),
        pltpu.VMEM((3, 256, WIDE), BF16),
        pltpu.VMEM((2, 2, 128, 128), F32),
        pltpu.VMEM((256, WIDE), BF16),
        pltpu.VMEM((8, 128), F32),
        pltpu.VMEM((2, 8, 16, D), BF16),
        pltpu.VMEM((256, D), BF16),
        pltpu.VMEM((3, 256, WIDE), BF16),
        pltpu.VMEM((2, 2, 4, 16, D), BF16),
        pltpu.VMEM((2, 4, 16, D), BF16),
        pltpu.VMEM((2, 4, 16, D), BF16),
        pltpu.VMEM((2, 4, 16, D), BF16),
        pltpu.VMEM((2, 16, D), BF16),
        pltpu.VMEM((4, 4, 4, ROWS, WIDE), BF16),
        pltpu.VMEM((4, 3, 4, ROWS, WIDE), BF16),
        pltpu.VMEM((4, 4, ROWS, WIDE), F32),
        pltpu.VMEM((4, 4, ROWS, WIDE), BF16),
        pltpu.VMEM((4, 3, ROWS, WIDE), BF16),
        pltpu.VMEM((2, D), F32),
        pltpu.VMEM((8, 2, D), F32),
        pltpu.VMEM((16, 2, D), F32),
        pltpu.VMEM((2, D), F32),
        dma((4, 15)), dma((4, 16)),
        dma((7,)), dma((8,)),
        dma((2, 7)), dma((2, 8)),
        dma((2, 5)), dma((2, 5)),
        dma((4, 6)), dma((4, 6)),
        dma((8,)), dma((8,)),
        dma((16,)), dma((16,)),
    ]
    outs = pl.pallas_call(
        kernel,
        out_shape=(
            jax.ShapeDtypeStruct((2, 16, D), BF16),
            shard,
            shard,
            shard,
            jax.ShapeDtypeStruct((2, D), F32),
        ),
        in_specs=[vmem] * 7,
        out_specs=(vmem,) * 5,
        scratch_shapes=scratch,
        compiler_params=pltpu.CompilerParams(
            collective_id=0, has_side_effects=True, vmem_limit_bytes=56 * 1024 * 1024
        ),
        cost_estimate=pl.CostEstimate(flops=3 * 10**9, bytes_accessed=10**7, transcendentals=10**5),
    )(
        x_in.reshape(2, 16, D),
        out_grad.reshape(2, 8, 16, D),
        layer_scale,
        norm_gain,
        master[0],
        moment_one[0],
        moment_two[0],
    )
    grads, new_master, first, second, scales = outs
    return (grads.reshape(1, 2, 1, 16, D), new_master[None], first[None], second[None], scales[None])


def solution(mesh):
    placed = (
        P("pipe", None, "dp", "tensor", None),
        P(None, "dp", None, None),
        P("pipe", None),
        P("pipe", None),
        P("pipe", "dp", "tensor"),
        P("pipe", "dp", "tensor"),
        P("pipe", "dp", "tensor"),
    )
    return jax.shard_map(
        local,
        mesh=mesh,
        in_specs=placed,
        out_specs=(
            P("pipe", None, "dp", "tensor", None),
            P("pipe", "dp", "tensor"),
            P("pipe", "dp", "tensor"),
            P("pipe", "dp", "tensor"),
            P("pipe", None, None),
        ),
        check_vma=False,
    )
```

```python
import functools
import math

import jax
import jax.numpy as jnp
from jax import lax
from jax.experimental import pallas as pl
from jax.experimental.pallas import tpu as pltpu
from jax.sharding import PartitionSpec as P

HD = 128
D = 1600
ROWS = 100
WIDE = 256
SIDE = 4

beta_one = 0.9
beta_two = 0.95
adam_eps = 1e-08
learn_rate = 0.001
weight_decay = 0.05
adam_step = 100.0
norm_eps = 1e-06

F32 = jnp.float32
BF16 = jnp.bfloat16
MESH = pl.DeviceIdType.MESH


def dot(left, right, dims):
    return lax.dot_general(left, right, ((dims[:1], dims[1:]), ((), ())), preferred_element_type=F32)


def kernel(
    x_ref, og_ref, ls_ref, gain_ref, master_ref,
    ig_ref, grad_ref, sg_ref,
    wload, wland, dense, wide, xall, normed, flat, qkv, probs, att, inc, scaled, dproj,
    part, s1land, arrived, passing, running, own_out, gsend, gland1, gmid, gmid_send, gland2, small, sm_t, sm_d, sm_send,
    m_s, w_ss, w_rs, x_ss, x_rs, a_ss, a_rs, c_ss, c_rs, r_ss, r_rs, o_ss, o_rs, g_ss, g_rs, t_ss, t_rs, d_ss, d_rs,
):
    p = lax.axis_index("pipe")
    r = lax.axis_index("dp")
    t = lax.axis_index("tensor")
    chip = t // 2
    core = t % 2
    y = r // SIDE
    x = r % SIDE
    partner = chip * 2 + (1 - core)
    mirror = (3 - chip) * 2 + core
    root = math.sqrt(HD)

    def up(v, by):
        return lax.rem(v + by, SIDE)

    def send(src, dst, ss, rs, where):
        copy = pltpu.make_async_remote_copy(
            src_ref=src, dst_ref=dst, send_sem=ss, recv_sem=rs, device_id=where, device_id_type=MESH
        )
        copy.start()
        return copy

    def landed(dst, rs):
        pltpu.make_async_remote_copy(
            src_ref=dst, dst_ref=dst, send_sem=rs, recv_sem=rs,
            device_id={"tensor": partner}, device_id_type=MESH,
        ).wait_recv()

    loads = []
    for b in range(8):
        loads.append(pltpu.make_async_copy(master_ref.at[:, b], wload.at[b], m_s.at[b]))
        loads[b].start()

    barrier = pltpu.get_barrier_semaphore()
    for k in range(1, 16):
        pl.semaphore_signal(barrier, inc=1, device_id={"dp": lax.rem(r + k, 16)}, device_id_type=MESH)
    for k in range(1, 8):
        pl.semaphore_signal(barrier, inc=1, device_id={"tensor": lax.rem(t + k, 8)}, device_id_type=MESH)
    for k in (1, 3):
        pl.semaphore_signal(
            barrier, inc=1, device_id={"pipe": lax.rem(p + k, 4), "tensor": mirror}, device_id_type=MESH
        )
    for q in range(4):
        loads[2 * q].wait()
        loads[2 * q + 1].wait()
        wland[q, r] = jnp.concatenate([wload[2 * q], wload[2 * q + 1]], axis=1).astype(BF16)
    pl.semaphore_wait(barrier, 24)

    def at(h, near, far):
        return far * SIDE + near if h == 0 else near * SIDE + far

    def coords(h):
        return (x, y) if h == 0 else (y, x)

    def spread(buf, ss, rs):
        copies = [send(buf.at[t], buf.at[t], ss.at[0], rs.at[t], {"tensor": partner})]
        for k in range(1, 4):
            other = up(chip, k) * 2 + core
            copies.append(send(buf.at[t], buf.at[t], ss.at[k], rs.at[t], {"tensor": other}))
        return copies

    def relay(buf, ss, rs):
        copies = []
        for k in range(1, 4):
            other = up(chip, k) * 2 + core
            landed(buf.at[other], rs.at[other])
            copies.append(send(buf.at[other], buf.at[other], ss.at[3 + k], rs.at[other], {"tensor": partner}))
        return copies

    def settle(buf, rs):
        landed(buf.at[partner], rs.at[partner])
        for k in range(1, 4):
            other = up(chip, k) * 2 + 1 - core
            landed(buf.at[other], rs.at[other])

    pending = []

    def wsend(q, s, slot, where):
        pending.append(send(wland.at[q, s], wland.at[q, s], w_ss.at[q, slot], w_rs.at[q, s], {"dp": where}))

    for h in range(2):
        near, far = coords(h)
        for q in (2 * h, 2 * h + 1):
            wsend(q, r, 0, at(h, up(near, 1), far))
            wsend(q, r, 1, at(h, up(near, 3), far))
    xall[t] = x_ref[...]
    x_copies = spread(xall, x_ss, x_rs)
    for h in range(2):
        near, far = coords(h)
        for q in (2 * h, 2 * h + 1):
            wsend(q, r, 3, at(h, near, up(far, 1)))
            wsend(q, r, 4, at(h, near, up(far, 3)))
    for h in range(2):
        near, far = coords(h)
        for q in (2 * h, 2 * h + 1):
            below = at(h, up(near, 3), far)
            above = at(h, up(near, 1), far)
            landed(wland.at[q, below], w_rs.at[q, below])
            if q % 2 == 0:
                wsend(q, below, 2, above)
            landed(wland.at[q, above], w_rs.at[q, above])
            if q % 2 == 1:
                wsend(q, above, 2, below)
            for j, s in ((1, below), (2, above)):
                wsend(q, s, 3 + 3 * j, at(h, near, up(far, 1)))
                wsend(q, s, 4 + 3 * j, at(h, near, up(far, 3)))
    for h in range(2):
        near, far = coords(h)
        for q in (2 * h, 2 * h + 1):
            s = at(h, up(near, 2), far)
            landed(wland.at[q, s], w_rs.at[q, s])
            wsend(q, s, 12, at(h, near, up(far, 1)))
            wsend(q, s, 13, at(h, near, up(far, 3)))
    for j, step in enumerate((0, 3, 1, 2)):
        for h in range(2):
            near, far = coords(h)
            for q in (2 * h, 2 * h + 1):
                lower = at(h, up(near, step), up(far, 3))
                upper = at(h, up(near, step), up(far, 1))
                landed(wland.at[q, lower], w_rs.at[q, lower])
                if q % 2 == 0:
                    wsend(q, lower, 5 + 3 * j, at(h, near, up(far, 1)))
                landed(wland.at[q, upper], w_rs.at[q, upper])
                if q % 2 == 1:
                    wsend(q, upper, 5 + 3 * j, at(h, near, up(far, 3)))
    x_copies += relay(xall, x_ss, x_rs)
    settle(xall, x_rs)

    gain = gain_ref[...]
    for m in range(2):
        rows = xall[:, m].reshape(128, D).astype(F32)
        inverse = lax.rsqrt(jnp.mean(rows * rows, axis=-1, keepdims=True) + norm_eps)
        normed[m * 128 : (m + 1) * 128] = (rows * inverse * gain).astype(BF16)

    @pl.when(p == 3)
    def _():
        for m in range(2):
            inc[m] = og_ref[m].T.reshape(8, 16, D)

    flat[...] = normed[...].T

    for h in range(2):
        near, far = coords(h)
        for q in (2 * h, 2 * h + 1):
            for step in range(4):
                s = at(h, up(near, step), up(far, 2))
                landed(wland.at[q, s], w_rs.at[q, s])

    for q in range(4):
        for s in range(16):
            wide[s * ROWS : (s + 1) * ROWS] = wland[q, s].astype(F32)
        dense[q] = wide[...].astype(BF16)
        if q < 3:
            qkv[q] = dot(normed[...], dense[q], (1, 0)).astype(BF16)
    for m in range(2):
        row = slice(m * 128, (m + 1) * 128)
        for head in range(2):
            col = slice(head * HD, (head + 1) * HD)
            scores = dot(qkv[0, row, col], qkv[1, row, col], (1, 1)) / root
            scores = jnp.exp(scores - jnp.max(scores, axis=-1, keepdims=True))
            prob = scores / jnp.sum(scores, axis=-1, keepdims=True)
            probs[m, head] = prob
            att[row, col] = dot(prob.astype(BF16), qkv[2, row, col], (1, 0)).astype(BF16)

    def backward(m):
        row = slice(m * 128, (m + 1) * 128)
        scaled_now = (ls_ref[...] * inc[m].reshape(128, D).astype(F32)).astype(BF16)
        scaled[row] = scaled_now
        d_att = dot(scaled_now, dense[3], (1, 0)).astype(BF16)
        for head in range(2):
            col = slice(head * HD, (head + 1) * HD)
            d_now = d_att[:, col]
            d_prob = dot(d_now, qkv[2, row, col], (1, 1))
            delta = jnp.sum(d_now.astype(F32) * att[row, col].astype(F32), axis=-1, keepdims=True)
            prob = probs[m, head]
            d_score = (prob * (d_prob - delta) / root).astype(BF16)
            dproj[0, row, col] = dot(d_score, qkv[1, row, col], (1, 0)).astype(BF16)
            dproj[1, row, col] = dot(d_score, qkv[0, row, col], (0, 0)).astype(BF16)
            dproj[2, row, col] = dot(prob.astype(BF16), d_now, (0, 0)).astype(BF16)
        total = dot(dproj[0, row], dense[0], (1, 1))
        total += dot(dproj[1, row], dense[1], (1, 1))
        total += dot(dproj[2, row], dense[2], (1, 1))
        total = total.astype(BF16)
        for other in range(8):
            part[m, other % 2, other // 2] = total[other * 16 : (other + 1) * 16]

    def scale_part(m):
        row = slice(m * 128, (m + 1) * 128)
        out_rows = dot(att[row], dense[3], (1, 1))
        return jnp.sum(inc[m].reshape(128, D).astype(F32) * out_rows, axis=0, keepdims=True)

    def remote(src, dst, ss, rs, to):
        return pltpu.make_async_remote_copy(
            src_ref=src, dst_ref=dst, send_sem=ss, recv_sem=rs, device_id=to, device_id_type=MESH
        )

    below = {"tensor": lax.rem(t + 6, 8)}
    section_below = {"pipe": lax.rem(p + 3, 4), "tensor": mirror}

    def first_stage(m):
        return remote(part.at[m, 1 - core], s1land.at[m], c_ss.at[m], c_rs.at[m], {"tensor": partner})

    def across(m, j):
        i = 2 * j + core
        return remote(inc.at[m, i], inc.at[m, i], a_ss.at[m, j], a_rs.at[m, i], {"tensor": partner})

    def down(m, j):
        i = 2 * j + core
        return remote(inc.at[m, i], inc.at[m, i], a_ss.at[m, 4 + j], a_rs.at[m, i], below)

    def sum_down(m, j):
        return remote(passing.at[m, j], arrived.at[m, j], r_ss.at[m, j], r_rs.at[m, j], below)

    def hand_on(m, j):
        return remote(passing.at[m, j], inc.at[m, 2 * j + core], r_ss.at[m, j], a_rs.at[m, 2 * j + core], section_below)

    def give_back(m, j):
        return remote(passing.at[m, j], own_out.at[m], o_ss.at[m, j], o_rs.at[m], {"tensor": 2 * j + core})

    def take_piece(m, j):
        landed(inc.at[m, 2 * j + core], a_rs.at[m, 2 * j + core])

        @pl.when(chip > 0)
        def _():
            down(m, j).start()

        across(m, j).start()

    def take_rest(m):
        for j in range(4):
            landed(inc.at[m, 2 * j + 1 - core], a_rs.at[m, 2 * j + 1 - core])

    def reduce_start(m):
        landed(s1land.at[m], c_rs.at[m])

    def reduce_piece(m, j):
        running[...] = part[m, core, j].astype(F32) + s1land[m, j].astype(F32)

        @pl.when(chip < 3)
        def _():
            landed(arrived.at[m, j], r_rs.at[m, j])
            running[...] += arrived[m, j].astype(F32)

        @pl.when(chip > 0)
        def _():
            passing[m, j] = running[...].astype(BF16)
            sum_down(m, j).start()

        @pl.when(chip == 0)
        def _():
            i = 2 * j + core
            total = running[...]
            rows = xall[i, m].astype(F32)
            inverse = lax.rsqrt(jnp.mean(rows * rows, axis=-1, keepdims=True) + norm_eps)
            unit = rows * inverse
            e = total * gain
            d_input = inverse * (e - unit * jnp.mean(e * unit, axis=-1, keepdims=True))
            passing[m, j] = (inc[m, i].astype(F32) + d_input).astype(BF16)

            @pl.when(p > 0)
            def _():
                hand_on(m, j).start()

            if j > 0:
                give_back(m, j).start()
            small[1:2] += jnp.sum(total * unit, axis=0, keepdims=True)

    def gcopy(q, kind, second):
        near, far = coords(q // 2)
        ahead, back = (1, 3) if q % 2 == 0 else (3, 1)
        where = back if kind == 1 else ahead
        owner = (2, back, ahead)[kind]
        if second:
            to = at(q // 2, up(near, where), far)
            src, slot, land = gmid_send.at[q, up(near, owner)], 3 + kind, gland2.at[q, kind]
        else:
            to = at(q // 2, near, up(far, where))
            src, slot, land = gsend.at[q, up(far, owner)], kind, gland1.at[q, kind]
        return pltpu.make_async_remote_copy(
            src_ref=src, dst_ref=land, send_sem=g_ss.at[q, slot], recv_sem=g_rs.at[q, slot],
            device_id={"dp": to}, device_id_type=MESH,
        )

    order = (3, 0, 1, 2)

    def weight_grads():
        for q in order:
            if q == 3:
                wide[...] = dot(scaled[...], att[...], (0, 0))
            else:
                wide[...] = dot(flat[...], dproj[q], (1, 0))
            for s in range(16):
                place = s if q < 2 else (s % SIDE) * SIDE + s // SIDE
                gsend[q, place // SIDE, place % SIDE] = wide[s * ROWS : (s + 1) * ROWS].astype(BF16)
            gcopy(q, 0, False).start()
            gcopy(q, 1, False).start()

    small[...] = jnp.zeros((2, D), F32)

    @pl.when(p == 3)
    def _():
        for m in range(2):
            backward(m)
            first_stage(m).start()
        reduce_start(0)
        for j in range(4):
            reduce_piece(0, j)

    @pl.when(p < 3)
    def _():
        for j in range(4):
            take_piece(0, j)
        take_rest(0)
        backward(0)
        first_stage(0).start()
        reduce_start(0)
        for j in range(4):
            reduce_piece(0, j)
        for j in range(4):
            take_piece(1, j)
        take_rest(1)
        backward(1)
        first_stage(1).start()

        @pl.when(p == 0)
        def _():
            weight_grads()

    reduce_start(1)
    for j in range(4):
        reduce_piece(1, j)

    small[0:1] = scale_part(0) + scale_part(1)
    for k in range(1, 8):
        other = lax.rem(t + k, 8)
        pending.append(send(small, sm_t.at[t], t_ss.at[k], t_rs.at[t], {"tensor": other}))

    @pl.when(p > 0)
    def _():
        weight_grads()

    for q in order:
        near, far = coords(q // 2)
        line = up(far, 1 if q % 2 == 0 else 3)
        landed(gland1.at[q, 0], g_rs.at[q, 0])
        gsend[q, line] = (gsend[q, line].astype(F32) + gland1[q, 0].astype(F32)).astype(BF16)
        gcopy(q, 2, False).start()

    total = small[...]
    for k in range(1, 8):
        other = lax.rem(t + k, 8)
        landed(sm_t.at[other], t_rs.at[other])
        total += sm_t[other]
    sm_send[...] = total
    for k in range(1, 16):
        other = lax.rem(r + k, 16)
        pending.append(send(sm_send, sm_d.at[r], d_ss.at[k], d_rs.at[r], {"dp": other}))

    for q in order:
        near, far = coords(q // 2)
        landed(gland1.at[q, 1], g_rs.at[q, 1])
        landed(gland1.at[q, 2], g_rs.at[q, 2])
        gmid[q] = gsend[q, far].astype(F32) + gland1[q, 1].astype(F32) + gland1[q, 2].astype(F32)
        gmid_send[q] = gmid[q].astype(BF16)
        gcopy(q, 0, True).start()
        gcopy(q, 1, True).start()
    for q in order:
        near, far = coords(q // 2)
        line = up(near, 1 if q % 2 == 0 else 3)
        landed(gland2.at[q, 0], g_rs.at[q, 3])
        gmid_send[q, line] = (gmid[q, line] + gland2[q, 0].astype(F32)).astype(BF16)
        gcopy(q, 2, True).start()
    for q in order:
        near, far = coords(q // 2)
        landed(gland2.at[q, 1], g_rs.at[q, 4])
        landed(gland2.at[q, 2], g_rs.at[q, 5])
        grad_ref[:, q * WIDE : (q + 1) * WIDE] = (
            gmid[q, near] + gland2[q, 1].astype(F32) + gland2[q, 2].astype(F32)
        )

    total = sm_send[...]
    for k in range(1, 16):
        other = lax.rem(r + k, 16)
        landed(sm_d.at[other], d_rs.at[other])
        total += sm_d[other]
    sg_ref[...] = total

    for copy in pending + x_copies:
        copy.wait_send()
    for q in order:
        for kind in range(3):
            gcopy(q, kind, False).wait_send()
            gcopy(q, kind, True).wait_send()

    for m in range(2):
        first_stage(m).wait_send()

        @pl.when(p < 3)
        def _():
            for j in range(4):
                across(m, j).wait_send()

                @pl.when(chip > 0)
                def _():
                    down(m, j).wait_send()

        @pl.when(chip > 0)
        def _():
            for j in range(4):
                sum_down(m, j).wait_send()
            landed(own_out.at[m], o_rs.at[m])
            ig_ref[m] = own_out[m]

        @pl.when(chip == 0)
        def _():
            ig_ref[m] = passing[m, 0]
            for j in range(1, 4):
                give_back(m, j).wait_send()

            @pl.when(p > 0)
            def _():
                for j in range(4):
                    hand_on(m, j).wait_send()


def local(x_in, out_grad, layer_scale, norm_gain, master, moment_one, moment_two):
    vmem = pl.BlockSpec(memory_space=pltpu.VMEM)
    dma = pltpu.SemaphoreType.DMA
    scratch = [
        pltpu.VMEM((8, ROWS, 128), F32),
        pltpu.VMEM((4, 16, ROWS, WIDE), BF16),
        pltpu.VMEM((4, D, WIDE), BF16),
        pltpu.VMEM((D, WIDE), F32),
        pltpu.VMEM((8, 2, 16, D), BF16),
        pltpu.VMEM((256, D), BF16),
        pltpu.VMEM((D, 256), BF16),
        pltpu.VMEM((3, 256, WIDE), BF16),
        pltpu.VMEM((2, 2, 128, 128), F32),
        pltpu.VMEM((256, WIDE), BF16),
        pltpu.VMEM((2, 8, 16, D), BF16),
        pltpu.VMEM((256, D), BF16),
        pltpu.VMEM((3, 256, WIDE), BF16),
        pltpu.VMEM((2, 2, 4, 16, D), BF16),
        pltpu.VMEM((2, 4, 16, D), BF16),
        pltpu.VMEM((2, 4, 16, D), BF16),
        pltpu.VMEM((2, 4, 16, D), BF16),
        pltpu.VMEM((16, D), F32),
        pltpu.VMEM((2, 16, D), BF16),
        pltpu.VMEM((4, 4, 4, ROWS, WIDE), BF16),
        pltpu.VMEM((4, 3, 4, ROWS, WIDE), BF16),
        pltpu.VMEM((4, 4, ROWS, WIDE), F32),
        pltpu.VMEM((4, 4, ROWS, WIDE), BF16),
        pltpu.VMEM((4, 3, ROWS, WIDE), BF16),
        pltpu.VMEM((2, D), F32),
        pltpu.VMEM((8, 2, D), F32),
        pltpu.VMEM((16, 2, D), F32),
        pltpu.VMEM((2, D), F32),
        dma((8,)),
        dma((4, 15)), dma((4, 16)),
        dma((7,)), dma((8,)),
        dma((2, 8)), dma((2, 8)),
        dma((2,)), dma((2,)),
        dma((2, 4)), dma((2, 4)),
        dma((2, 4)), dma((2,)),
        dma((4, 6)), dma((4, 6)),
        dma((8,)), dma((8,)),
        dma((16,)), dma((16,)),
    ]
    grads, weight_grad, scales = pl.pallas_call(
        kernel,
        out_shape=(
            jax.ShapeDtypeStruct((2, 16, D), BF16),
            jax.ShapeDtypeStruct((ROWS, 4 * WIDE), F32),
            jax.ShapeDtypeStruct((2, D), F32),
        ),
        in_specs=[vmem] * 4 + [pl.BlockSpec(memory_space=pl.ANY)],
        out_specs=(vmem,) * 3,
        scratch_shapes=scratch,
        compiler_params=pltpu.CompilerParams(
            collective_id=0, has_side_effects=True, vmem_limit_bytes=56 * 1024 * 1024
        ),
        cost_estimate=pl.CostEstimate(flops=3 * 10**9, bytes_accessed=10**7, transcendentals=10**5),
    )(
        x_in.reshape(2, 16, D),
        out_grad.reshape(2, 128, D).transpose(0, 2, 1),
        layer_scale,
        norm_gain,
        master.reshape(ROWS, 8, 128),
    )
    bias_one = 1.0 - beta_one**adam_step
    bias_two = 1.0 - beta_two**adam_step
    first = beta_one * moment_one[0] + (1.0 - beta_one) * weight_grad
    second = beta_two * moment_two[0] + (1.0 - beta_two) * weight_grad * weight_grad
    update = first / bias_one / (jnp.sqrt(second / bias_two) + adam_eps)
    new_master = master[0] - learn_rate * (update + weight_decay * master[0])
    return (grads.reshape(1, 2, 1, 16, D), new_master[None], first[None], second[None], scales[None])


def solution(mesh):
    placed = (
        P("pipe", None, "dp", "tensor", None),
        P(None, "dp", None, None),
        P("pipe", None),
        P("pipe", None),
        P("pipe", "dp", "tensor"),
        P("pipe", "dp", "tensor"),
        P("pipe", "dp", "tensor"),
    )
    return jax.shard_map(
        local,
        mesh=mesh,
        in_specs=placed,
        out_specs=(
            P("pipe", None, "dp", "tensor", None),
            P("pipe", "dp", "tensor"),
            P("pipe", "dp", "tensor"),
            P("pipe", "dp", "tensor"),
            P("pipe", None, None),
        ),
        check_vma=False,
    )
```

```python
import functools
import math

import jax
import jax.numpy as jnp
from jax import lax
from jax.experimental import pallas as pl
from jax.experimental.pallas import tpu as pltpu
from jax.sharding import PartitionSpec as P

HD = 128
LEFT = 896
D = 1600
ROWS = 100
WIDE = 256
SIDE = 4

beta_one = 0.9
beta_two = 0.95
adam_eps = 1e-08
learn_rate = 0.001
weight_decay = 0.05
adam_step = 100.0
norm_eps = 1e-06

F32 = jnp.float32
BF16 = jnp.bfloat16
MESH = pl.DeviceIdType.MESH


def dot(left, right, dims):
    return lax.dot_general(left, right, ((dims[:1], dims[1:]), ((), ())), preferred_element_type=F32)


def kernel(
    x_ref, og_ref, ls_ref, gain_ref, master_ref,
    ig_ref, grad_ref, sg_ref,
    wload, wland, dense, wide, xall, normed, flat, qkv, probs, att, inc_l, inc_r, scaled, dproj,
    part, s1land, arrived_l, arrived_r, passing_l, passing_r, passing, running, own_out, gsend, gland1, gmid, gmid_send, gland2, small, sm_t, sm_d, sm_send,
    m_s, w_ss, w_rs, x_ss, x_rs, a_ss, a_rs, c_ss, c_rs, r_ss, r_rs, o_ss, o_rs, g_ss, g_rs, t_ss, t_rs, d_ss, d_rs,
):
    p = lax.axis_index("pipe")
    r = lax.axis_index("dp")
    t = lax.axis_index("tensor")
    chip = t // 2
    core = t % 2
    y = r // SIDE
    x = r % SIDE
    partner = chip * 2 + (1 - core)
    mirror = (3 - chip) * 2 + core
    root = math.sqrt(HD)

    def up(v, by):
        return lax.rem(v + by, SIDE)

    def send(src, dst, ss, rs, where):
        copy = pltpu.make_async_remote_copy(
            src_ref=src, dst_ref=dst, send_sem=ss, recv_sem=rs, device_id=where, device_id_type=MESH
        )
        copy.start()
        return copy

    def landed(dst, rs):
        pltpu.make_async_remote_copy(
            src_ref=dst, dst_ref=dst, send_sem=rs, recv_sem=rs,
            device_id={"tensor": partner}, device_id_type=MESH,
        ).wait_recv()

    loads = []
    for b in range(8):
        loads.append(pltpu.make_async_copy(master_ref.at[:, b], wload.at[b], m_s.at[b]))
        loads[b].start()

    barrier = pltpu.get_barrier_semaphore()
    for k in range(1, 16):
        pl.semaphore_signal(barrier, inc=1, device_id={"dp": lax.rem(r + k, 16)}, device_id_type=MESH)
    for k in range(1, 8):
        pl.semaphore_signal(barrier, inc=1, device_id={"tensor": lax.rem(t + k, 8)}, device_id_type=MESH)
    for k in (1, 3):
        pl.semaphore_signal(
            barrier, inc=1, device_id={"pipe": lax.rem(p + k, 4), "tensor": mirror}, device_id_type=MESH
        )
    for q in range(4):
        loads[2 * q].wait()
        loads[2 * q + 1].wait()
        wland[q // 2, r, q % 2] = jnp.concatenate([wload[2 * q], wload[2 * q + 1]], axis=1).astype(BF16)
    pl.semaphore_wait(barrier, 24)

    def at(h, near, far):
        return far * SIDE + near if h == 0 else near * SIDE + far

    def coords(h):
        return (x, y) if h == 0 else (y, x)

    def spread(buf, ss, rs):
        copies = [send(buf.at[t], buf.at[t], ss.at[0], rs.at[t], {"tensor": partner})]
        for k in range(1, 4):
            other = up(chip, k) * 2 + core
            copies.append(send(buf.at[t], buf.at[t], ss.at[k], rs.at[t], {"tensor": other}))
        return copies

    def relay(buf, ss, rs):
        copies = []
        for k in range(1, 4):
            other = up(chip, k) * 2 + core
            landed(buf.at[other], rs.at[other])
            copies.append(send(buf.at[other], buf.at[other], ss.at[3 + k], rs.at[other], {"tensor": partner}))
        return copies

    def settle(buf, rs):
        landed(buf.at[partner], rs.at[partner])
        for k in range(1, 4):
            other = up(chip, k) * 2 + 1 - core
            landed(buf.at[other], rs.at[other])

    pending = []

    def wpair(h, s, slot, where):
        pending.append(send(wland.at[h, s], wland.at[h, s], w_ss.at[h, slot], w_rs.at[h, s, 0], {"dp": where}))

    def wone(h, s, i, slot, where):
        pending.append(send(wland.at[h, s, i], wland.at[h, s, i], w_ss.at[h, slot], w_rs.at[h, s, i], {"dp": where}))

    for h in range(2):
        near, far = coords(h)
        wpair(h, r, 0, at(h, up(near, 1), far))
        wpair(h, r, 1, at(h, up(near, 3), far))
    xall[t] = x_ref[...]
    x_copies = spread(xall, x_ss, x_rs)
    for h in range(2):
        near, far = coords(h)
        wpair(h, r, 4, at(h, near, up(far, 1)))
        wpair(h, r, 5, at(h, near, up(far, 3)))
    for h in range(2):
        near, far = coords(h)
        below = at(h, up(near, 3), far)
        above = at(h, up(near, 1), far)
        landed(wland.at[h, below], w_rs.at[h, below, 0])
        wone(h, below, 0, 2, above)
        landed(wland.at[h, above], w_rs.at[h, above, 0])
        wone(h, above, 1, 3, below)
        for j, s in ((1, below), (2, above)):
            wpair(h, s, 4 + 4 * j, at(h, near, up(far, 1)))
            wpair(h, s, 5 + 4 * j, at(h, near, up(far, 3)))
    for h in range(2):
        near, far = coords(h)
        s = at(h, up(near, 2), far)
        for i in range(2):
            landed(wland.at[h, s, i], w_rs.at[h, s, i])
        wpair(h, s, 16, at(h, near, up(far, 1)))
        wpair(h, s, 17, at(h, near, up(far, 3)))

    for j, step in enumerate((0, 3, 1, 2)):
        for h in range(2):
            near, far = coords(h)
            lower = at(h, up(near, step), up(far, 3))
            upper = at(h, up(near, step), up(far, 1))
            landed(wland.at[h, lower], w_rs.at[h, lower, 0])
            wone(h, lower, 0, 6 + 4 * j, at(h, near, up(far, 1)))
            landed(wland.at[h, upper], w_rs.at[h, upper, 0])
            wone(h, upper, 1, 7 + 4 * j, at(h, near, up(far, 3)))
    x_copies += relay(xall, x_ss, x_rs)
    settle(xall, x_rs)

    gain = gain_ref[...]
    for m in range(2):
        rows = xall[:, m].reshape(128, D).astype(F32)
        inverse = lax.rsqrt(jnp.mean(rows * rows, axis=-1, keepdims=True) + norm_eps)
        normed[m * 128 : (m + 1) * 128] = (rows * inverse * gain).astype(BF16)

    @pl.when(p == 3)
    def _():
        for m in range(2):
            rows = og_ref[m].T.reshape(8, 16, D)
            inc_l[m] = rows[:, :, :LEFT]
            inc_r[m] = rows[:, :, LEFT:]

    flat[...] = normed[...].T

    for h in range(2):
        near, far = coords(h)
        for step in (0, 3, 1, 2):
            s = at(h, up(near, step), up(far, 2))
            for i in range(2):
                landed(wland.at[h, s, i], w_rs.at[h, s, i])

    for q in range(4):
        for s in range(16):
            wide[s * ROWS : (s + 1) * ROWS] = wland[q // 2, s, q % 2].astype(F32)
        dense[q] = wide[...].astype(BF16)
        if q < 3:
            qkv[q] = dot(normed[...], dense[q], (1, 0)).astype(BF16)
    for m in range(2):
        row = slice(m * 128, (m + 1) * 128)
        for head in range(2):
            col = slice(head * HD, (head + 1) * HD)
            scores = dot(qkv[0, row, col], qkv[1, row, col], (1, 1)) / root
            scores = jnp.exp(scores - jnp.max(scores, axis=-1, keepdims=True))
            prob = scores / jnp.sum(scores, axis=-1, keepdims=True)
            probs[m, head] = prob
            att[row, col] = dot(prob.astype(BF16), qkv[2, row, col], (1, 0)).astype(BF16)

    inc, arrived, parting = (inc_l, inc_r), (arrived_l, arrived_r), (passing_l, passing_r)

    def incoming(m):
        return jnp.concatenate([inc_l[m].reshape(128, LEFT), inc_r[m].reshape(128, D - LEFT)], axis=1).astype(F32)

    def backward(m):
        row = slice(m * 128, (m + 1) * 128)
        scaled_now = (ls_ref[...] * incoming(m)).astype(BF16)
        scaled[row] = scaled_now
        d_att = dot(scaled_now, dense[3], (1, 0)).astype(BF16)
        for head in range(2):
            col = slice(head * HD, (head + 1) * HD)
            d_now = d_att[:, col]
            d_prob = dot(d_now, qkv[2, row, col], (1, 1))
            delta = jnp.sum(d_now.astype(F32) * att[row, col].astype(F32), axis=-1, keepdims=True)
            prob = probs[m, head]
            d_score = (prob * (d_prob - delta) / root).astype(BF16)
            dproj[0, row, col] = dot(d_score, qkv[1, row, col], (1, 0)).astype(BF16)
            dproj[1, row, col] = dot(d_score, qkv[0, row, col], (0, 0)).astype(BF16)
            dproj[2, row, col] = dot(prob.astype(BF16), d_now, (0, 0)).astype(BF16)
        total = dot(dproj[0, row], dense[0], (1, 1))
        total += dot(dproj[1, row], dense[1], (1, 1))
        total += dot(dproj[2, row], dense[2], (1, 1))
        total = total.astype(BF16)
        for other in range(8):
            part[m, other % 2, other // 2] = total[other * 16 : (other + 1) * 16]

    def scale_part(m):
        row = slice(m * 128, (m + 1) * 128)
        out_rows = dot(att[row], dense[3], (1, 1))
        return jnp.sum(incoming(m) * out_rows, axis=0, keepdims=True)

    def remote(src, dst, ss, rs, to):
        return pltpu.make_async_remote_copy(
            src_ref=src, dst_ref=dst, send_sem=ss, recv_sem=rs, device_id=to, device_id_type=MESH
        )

    below = {"tensor": lax.rem(t + 6, 8)}
    section_below = {"pipe": lax.rem(p + 3, 4), "tensor": mirror}

    def first_stage(m):
        return remote(part.at[m, 1 - core], s1land.at[m], c_ss.at[m], c_rs.at[m], {"tensor": partner})

    def across(m, j, c):
        ref = inc[c].at[m, 2 * j + core]
        return remote(ref, ref, a_ss.at[m, c, j], a_rs.at[m, c, 2 * j + core], {"tensor": partner})

    def down(m, j, c):
        ref = inc[c].at[m, 2 * j + core]
        return remote(ref, ref, a_ss.at[m, c, 4 + j], a_rs.at[m, c, 2 * j + core], below)

    def sum_down(m, j, c):
        return remote(parting[c].at[m, j], arrived[c].at[m, j], r_ss.at[m, c, j], r_rs.at[m, c, j], below)

    def hand_on(m, j, c):
        i = 2 * j + core
        return remote(parting[c].at[m, j], inc[c].at[m, i], r_ss.at[m, c, j], a_rs.at[m, c, i], section_below)

    def give_back(m, j):
        return remote(passing.at[m, j], own_out.at[m], o_ss.at[m, j], o_rs.at[m], {"tensor": 2 * j + core})

    def take_piece(m, j):
        for c in range(2):
            landed(inc[c].at[m, 2 * j + core], a_rs.at[m, c, 2 * j + core])

            @pl.when(chip > 0)
            def _():
                down(m, j, c).start()

            across(m, j, c).start()

    def take_rest(m):
        for j in range(4):
            for c in range(2):
                landed(inc[c].at[m, 2 * j + 1 - core], a_rs.at[m, c, 2 * j + 1 - core])

    def reduce_start(m):
        landed(s1land.at[m], c_rs.at[m])

    def reduce_piece(m, j):
        for c, cols in enumerate((slice(0, LEFT), slice(LEFT, D))):
            own = part[m, core, j, :, cols].astype(F32) + s1land[m, j, :, cols].astype(F32)
            running[:, cols] = own

            @pl.when(chip < 3)
            def _():
                landed(arrived[c].at[m, j], r_rs.at[m, c, j])
                running[:, cols] = own + arrived[c][m, j].astype(F32)

            @pl.when(chip > 0)
            def _():
                parting[c][m, j] = running[:, cols].astype(BF16)
                sum_down(m, j, c).start()

        @pl.when(chip == 0)
        def _():
            i = 2 * j + core
            total = running[...]
            rows = xall[i, m].astype(F32)
            inverse = lax.rsqrt(jnp.mean(rows * rows, axis=-1, keepdims=True) + norm_eps)
            unit = rows * inverse
            e = total * gain
            d_input = inverse * (e - unit * jnp.mean(e * unit, axis=-1, keepdims=True))
            held = jnp.concatenate([inc_l[m, i], inc_r[m, i]], axis=1)
            passed = (held.astype(F32) + d_input).astype(BF16)
            passing_l[m, j] = passed[:, :LEFT]
            passing_r[m, j] = passed[:, LEFT:]

            @pl.when(p > 0)
            def _():
                for c in range(2):
                    hand_on(m, j, c).start()

            passing[m, j] = passed
            if j > 0:
                give_back(m, j).start()
            small[1:2] += jnp.sum(total * unit, axis=0, keepdims=True)

    def gcopy(q, kind, second):
        near, far = coords(q // 2)
        ahead, back = (1, 3) if q % 2 == 0 else (3, 1)
        where = back if kind == 1 else ahead
        owner = (2, back, ahead)[kind]
        if second:
            to = at(q // 2, up(near, where), far)
            src, slot, land = gmid_send.at[q, up(near, owner)], 3 + kind, gland2.at[q, kind]
        else:
            to = at(q // 2, near, up(far, where))
            src, slot, land = gsend.at[q, up(far, owner)], kind, gland1.at[q, kind]
        return pltpu.make_async_remote_copy(
            src_ref=src, dst_ref=land, send_sem=g_ss.at[q, slot], recv_sem=g_rs.at[q, slot],
            device_id={"dp": to}, device_id_type=MESH,
        )

    order = (3, 0, 1, 2)

    def weight_grads():
        for q in order:
            if q == 3:
                wide[...] = dot(scaled[...], att[...], (0, 0))
            else:
                wide[...] = dot(flat[...], dproj[q], (1, 0))
            for s in range(16):
                place = s if q < 2 else (s % SIDE) * SIDE + s // SIDE
                gsend[q, place // SIDE, place % SIDE] = wide[s * ROWS : (s + 1) * ROWS].astype(BF16)
            gcopy(q, 0, False).start()
            gcopy(q, 1, False).start()

    small[...] = jnp.zeros((2, D), F32)

    @pl.when(p == 3)
    def _():
        for m in range(2):
            backward(m)
            first_stage(m).start()
        reduce_start(0)
        for j in range(4):
            reduce_piece(0, j)

    @pl.when(p < 3)
    def _():
        for j in range(4):
            take_piece(0, j)
        take_rest(0)
        backward(0)
        first_stage(0).start()
        reduce_start(0)
        for j in range(4):
            reduce_piece(0, j)
        for j in range(4):
            take_piece(1, j)
        take_rest(1)
        backward(1)
        first_stage(1).start()

        @pl.when(p == 0)
        def _():
            weight_grads()

    reduce_start(1)
    for j in range(4):
        reduce_piece(1, j)

    small[0:1] = scale_part(0) + scale_part(1)
    for k in range(1, 8):
        other = lax.rem(t + k, 8)
        pending.append(send(small, sm_t.at[t], t_ss.at[k], t_rs.at[t], {"tensor": other}))

    @pl.when(p > 0)
    def _():
        weight_grads()

    for q in order:
        near, far = coords(q // 2)
        line = up(far, 1 if q % 2 == 0 else 3)
        landed(gland1.at[q, 0], g_rs.at[q, 0])
        gsend[q, line] = (gsend[q, line].astype(F32) + gland1[q, 0].astype(F32)).astype(BF16)
        gcopy(q, 2, False).start()

    total = small[...]
    for k in range(1, 8):
        other = lax.rem(t + k, 8)
        landed(sm_t.at[other], t_rs.at[other])
        total += sm_t[other]
    sm_send[...] = total
    for k in range(1, 16):
        other = lax.rem(r + k, 16)
        pending.append(send(sm_send, sm_d.at[r], d_ss.at[k], d_rs.at[r], {"dp": other}))

    for q in order:
        near, far = coords(q // 2)
        landed(gland1.at[q, 1], g_rs.at[q, 1])
        landed(gland1.at[q, 2], g_rs.at[q, 2])
        gmid[q] = gsend[q, far].astype(F32) + gland1[q, 1].astype(F32) + gland1[q, 2].astype(F32)
        gmid_send[q] = gmid[q].astype(BF16)
        gcopy(q, 0, True).start()
        gcopy(q, 1, True).start()
    for q in order:
        near, far = coords(q // 2)
        line = up(near, 1 if q % 2 == 0 else 3)
        landed(gland2.at[q, 0], g_rs.at[q, 3])
        gmid_send[q, line] = (gmid[q, line] + gland2[q, 0].astype(F32)).astype(BF16)
        gcopy(q, 2, True).start()
    for q in order:
        near, far = coords(q // 2)
        landed(gland2.at[q, 1], g_rs.at[q, 4])
        landed(gland2.at[q, 2], g_rs.at[q, 5])
        grad_ref[:, q * WIDE : (q + 1) * WIDE] = (
            gmid[q, near] + gland2[q, 1].astype(F32) + gland2[q, 2].astype(F32)
        )

    total = sm_send[...]
    for k in range(1, 16):
        other = lax.rem(r + k, 16)
        landed(sm_d.at[other], d_rs.at[other])
        total += sm_d[other]
    sg_ref[...] = total

    for copy in pending + x_copies:
        copy.wait_send()
    for q in order:
        for kind in range(3):
            gcopy(q, kind, False).wait_send()
            gcopy(q, kind, True).wait_send()

    for m in range(2):
        first_stage(m).wait_send()

        @pl.when(p < 3)
        def _():
            for j in range(4):
                for c in range(2):
                    across(m, j, c).wait_send()

            @pl.when(chip > 0)
            def _():
                for j in range(4):
                    for c in range(2):
                        down(m, j, c).wait_send()

        @pl.when(chip > 0)
        def _():
            for j in range(4):
                for c in range(2):
                    sum_down(m, j, c).wait_send()
            landed(own_out.at[m], o_rs.at[m])
            ig_ref[m] = own_out[m]

        @pl.when(chip == 0)
        def _():
            ig_ref[m] = passing[m, 0]
            for j in range(1, 4):
                give_back(m, j).wait_send()

            @pl.when(p > 0)
            def _():
                for j in range(4):
                    for c in range(2):
                        hand_on(m, j, c).wait_send()


def local(x_in, out_grad, layer_scale, norm_gain, master, moment_one, moment_two):
    vmem = pl.BlockSpec(memory_space=pltpu.VMEM)
    dma = pltpu.SemaphoreType.DMA
    scratch = [
        pltpu.VMEM((8, ROWS, 128), F32),
        pltpu.VMEM((2, 16, 2, ROWS, WIDE), BF16),
        pltpu.VMEM((4, D, WIDE), BF16),
        pltpu.VMEM((D, WIDE), F32),
        pltpu.VMEM((8, 2, 16, D), BF16),
        pltpu.VMEM((256, D), BF16),
        pltpu.VMEM((D, 256), BF16),
        pltpu.VMEM((3, 256, WIDE), BF16),
        pltpu.VMEM((2, 2, 128, 128), F32),
        pltpu.VMEM((256, WIDE), BF16),
        pltpu.VMEM((2, 8, 16, LEFT), BF16),
        pltpu.VMEM((2, 8, 16, D - LEFT), BF16),
        pltpu.VMEM((256, D), BF16),
        pltpu.VMEM((3, 256, WIDE), BF16),
        pltpu.VMEM((2, 2, 4, 16, D), BF16),
        pltpu.VMEM((2, 4, 16, D), BF16),
        pltpu.VMEM((2, 4, 16, LEFT), BF16),
        pltpu.VMEM((2, 4, 16, D - LEFT), BF16),
        pltpu.VMEM((2, 4, 16, LEFT), BF16),
        pltpu.VMEM((2, 4, 16, D - LEFT), BF16),
        pltpu.VMEM((2, 4, 16, D), BF16),
        pltpu.VMEM((16, D), F32),
        pltpu.VMEM((2, 16, D), BF16),
        pltpu.VMEM((4, 4, 4, ROWS, WIDE), BF16),
        pltpu.VMEM((4, 3, 4, ROWS, WIDE), BF16),
        pltpu.VMEM((4, 4, ROWS, WIDE), F32),
        pltpu.VMEM((4, 4, ROWS, WIDE), BF16),
        pltpu.VMEM((4, 3, ROWS, WIDE), BF16),
        pltpu.VMEM((2, D), F32),
        pltpu.VMEM((8, 2, D), F32),
        pltpu.VMEM((16, 2, D), F32),
        pltpu.VMEM((2, D), F32),
        dma((8,)),
        dma((2, 20)), dma((2, 16, 2)),
        dma((7,)), dma((8,)),
        dma((2, 2, 8)), dma((2, 2, 8)),
        dma((2,)), dma((2,)),
        dma((2, 2, 4)), dma((2, 2, 4)),
        dma((2, 4)), dma((2,)),
        dma((4, 6)), dma((4, 6)),
        dma((8,)), dma((8,)),
        dma((16,)), dma((16,)),
    ]
    grads, weight_grad, scales = pl.pallas_call(
        kernel,
        out_shape=(
            jax.ShapeDtypeStruct((2, 16, D), BF16),
            jax.ShapeDtypeStruct((ROWS, 4 * WIDE), F32),
            jax.ShapeDtypeStruct((2, D), F32),
        ),
        in_specs=[vmem] * 4 + [pl.BlockSpec(memory_space=pl.ANY)],
        out_specs=(vmem,) * 3,
        scratch_shapes=scratch,
        compiler_params=pltpu.CompilerParams(
            collective_id=0, has_side_effects=True, vmem_limit_bytes=56 * 1024 * 1024
        ),
        cost_estimate=pl.CostEstimate(flops=3 * 10**9, bytes_accessed=10**7, transcendentals=10**5),
    )(
        x_in.reshape(2, 16, D),
        out_grad.reshape(2, 128, D).transpose(0, 2, 1),
        layer_scale,
        norm_gain,
        master.reshape(ROWS, 8, 128),
    )
    bias_one = 1.0 - beta_one**adam_step
    bias_two = 1.0 - beta_two**adam_step
    first = beta_one * moment_one[0] + (1.0 - beta_one) * weight_grad
    second = beta_two * moment_two[0] + (1.0 - beta_two) * weight_grad * weight_grad
    update = first / bias_one / (jnp.sqrt(second / bias_two) + adam_eps)
    new_master = master[0] - learn_rate * (update + weight_decay * master[0])
    return (grads.reshape(1, 2, 1, 16, D), new_master[None], first[None], second[None], scales[None])


def solution(mesh):
    placed = (
        P("pipe", None, "dp", "tensor", None),
        P(None, "dp", None, None),
        P("pipe", None),
        P("pipe", None),
        P("pipe", "dp", "tensor"),
        P("pipe", "dp", "tensor"),
        P("pipe", "dp", "tensor"),
    )
    return jax.shard_map(
        local,
        mesh=mesh,
        in_specs=placed,
        out_specs=(
            P("pipe", None, "dp", "tensor", None),
            P("pipe", "dp", "tensor"),
            P("pipe", "dp", "tensor"),
            P("pipe", "dp", "tensor"),
            P("pipe", None, None),
        ),
        check_vma=False,
    )
```

```python
import functools
import math

import jax
import jax.numpy as jnp
from jax import lax
from jax.experimental import pallas as pl
from jax.experimental.pallas import tpu as pltpu
from jax.sharding import PartitionSpec as P

HD = 128
LEFT = 896
D = 1600
ROWS = 100
WIDE = 256
SIDE = 4

beta_one = 0.9
beta_two = 0.95
adam_eps = 1e-08
learn_rate = 0.001
weight_decay = 0.05
adam_step = 100.0
norm_eps = 1e-06

F32 = jnp.float32
BF16 = jnp.bfloat16
MESH = pl.DeviceIdType.MESH


def dot(left, right, dims):
    return lax.dot_general(left, right, ((dims[:1], dims[1:]), ((), ())), preferred_element_type=F32)


def kernel(
    x_ref, og_ref, ls_ref, gain_ref, master_ref,
    ig_ref, grad_ref, sg_ref,
    wload, wland, dense, wide, xall, normed, flat, qkv, probs, att, inc_l, inc_r, scaled, dproj,
    part, s1land, arrived_l, arrived_r, passing_l, passing_r, passing, running, own_out, gsend, gland1, gmid, gmid_send, gland2, small, sm_t, sm_d, sm_send,
    m_s, w_ss, w_rs, x_ss, x_rs, a_ss, a_rs, c_ss, c_rs, r_ss, r_rs, o_ss, o_rs, g_ss, g_rs, t_ss, t_rs, d_ss, d_rs,
):
    p = lax.axis_index("pipe")
    r = lax.axis_index("dp")
    t = lax.axis_index("tensor")
    chip = t // 2
    core = t % 2
    y = r // SIDE
    x = r % SIDE
    partner = chip * 2 + (1 - core)
    mirror = (3 - chip) * 2 + core
    root = math.sqrt(HD)

    def up(v, by):
        return lax.rem(v + by, SIDE)

    def send(src, dst, ss, rs, where):
        copy = pltpu.make_async_remote_copy(
            src_ref=src, dst_ref=dst, send_sem=ss, recv_sem=rs, device_id=where, device_id_type=MESH
        )
        copy.start()
        return copy

    def landed(dst, rs):
        pltpu.make_async_remote_copy(
            src_ref=dst, dst_ref=dst, send_sem=rs, recv_sem=rs,
            device_id={"tensor": partner}, device_id_type=MESH,
        ).wait_recv()

    loads = []
    for b in range(8):
        loads.append(pltpu.make_async_copy(master_ref.at[:, b], wload.at[b], m_s.at[b]))
        loads[b].start()

    barrier = pltpu.get_barrier_semaphore()
    for k in range(1, 16):
        pl.semaphore_signal(barrier, inc=1, device_id={"dp": lax.rem(r + k, 16)}, device_id_type=MESH)
    for k in range(1, 8):
        pl.semaphore_signal(barrier, inc=1, device_id={"tensor": lax.rem(t + k, 8)}, device_id_type=MESH)
    for k in (1, 3):
        pl.semaphore_signal(
            barrier, inc=1, device_id={"pipe": lax.rem(p + k, 4), "tensor": mirror}, device_id_type=MESH
        )
    for q in range(4):
        loads[2 * q].wait()
        loads[2 * q + 1].wait()
        wland[q // 2, r, q % 2] = jnp.concatenate([wload[2 * q], wload[2 * q + 1]], axis=1).astype(BF16)
    pl.semaphore_wait(barrier, 24)

    def at(h, near, far):
        return far * SIDE + near if h == 0 else near * SIDE + far

    def coords(h):
        return (x, y) if h == 0 else (y, x)

    def spread(buf, ss, rs):
        copies = [send(buf.at[t], buf.at[t], ss.at[0], rs.at[t], {"tensor": partner})]
        for k in range(1, 4):
            other = up(chip, k) * 2 + core
            copies.append(send(buf.at[t], buf.at[t], ss.at[k], rs.at[t], {"tensor": other}))
        return copies

    def relay(buf, ss, rs):
        copies = []
        for k in range(1, 4):
            other = up(chip, k) * 2 + core
            landed(buf.at[other], rs.at[other])
            copies.append(send(buf.at[other], buf.at[other], ss.at[3 + k], rs.at[other], {"tensor": partner}))
        return copies

    def settle(buf, rs):
        landed(buf.at[partner], rs.at[partner])
        for k in range(1, 4):
            other = up(chip, k) * 2 + 1 - core
            landed(buf.at[other], rs.at[other])

    pending = []

    def wpair(h, s, slot, where):
        pending.append(send(wland.at[h, s], wland.at[h, s], w_ss.at[h, slot], w_rs.at[h, s, 0], {"dp": where}))

    def wone(h, s, i, slot, where):
        pending.append(send(wland.at[h, s, i], wland.at[h, s, i], w_ss.at[h, slot], w_rs.at[h, s, i], {"dp": where}))

    for h in range(2):
        near, far = coords(h)
        wpair(h, r, 0, at(h, up(near, 1), far))
        wpair(h, r, 1, at(h, up(near, 3), far))
    xall[t] = x_ref[...]
    x_copies = spread(xall, x_ss, x_rs)
    for h in range(2):
        near, far = coords(h)
        wpair(h, r, 4, at(h, near, up(far, 1)))
        wpair(h, r, 5, at(h, near, up(far, 3)))
    for h in range(2):
        near, far = coords(h)
        below = at(h, up(near, 3), far)
        above = at(h, up(near, 1), far)
        landed(wland.at[h, below], w_rs.at[h, below, 0])
        wone(h, below, 0, 2, above)
        landed(wland.at[h, above], w_rs.at[h, above, 0])
        wone(h, above, 1, 3, below)
        for j, s in ((1, below), (2, above)):
            wpair(h, s, 4 + 4 * j, at(h, near, up(far, 1)))
            wpair(h, s, 5 + 4 * j, at(h, near, up(far, 3)))
    for h in range(2):
        near, far = coords(h)
        s = at(h, up(near, 2), far)
        for i in range(2):
            landed(wland.at[h, s, i], w_rs.at[h, s, i])
        wpair(h, s, 16, at(h, near, up(far, 1)))
        wpair(h, s, 17, at(h, near, up(far, 3)))

    for j, step in enumerate((0, 3, 1, 2)):
        for h in range(2):
            near, far = coords(h)
            lower = at(h, up(near, step), up(far, 3))
            upper = at(h, up(near, step), up(far, 1))
            landed(wland.at[h, lower], w_rs.at[h, lower, 0])
            wone(h, lower, 0, 6 + 4 * j, at(h, near, up(far, 1)))
            landed(wland.at[h, upper], w_rs.at[h, upper, 0])
            wone(h, upper, 1, 7 + 4 * j, at(h, near, up(far, 3)))
    x_copies += relay(xall, x_ss, x_rs)
    settle(xall, x_rs)

    gain = gain_ref[...]
    for m in range(2):
        rows = xall[:, m].reshape(128, D).astype(F32)
        inverse = lax.rsqrt(jnp.mean(rows * rows, axis=-1, keepdims=True) + norm_eps)
        normed[m * 128 : (m + 1) * 128] = (rows * inverse * gain).astype(BF16)

    @pl.when(p == 3)
    def _():
        for m in range(2):
            rows = og_ref[m].T.reshape(8, 16, D)
            inc_l[m] = rows[:, :, :LEFT]
            inc_r[m] = rows[:, :, LEFT:]

    flat[...] = normed[...].T

    for h in range(2):
        near, far = coords(h)
        for step in (0, 3, 1, 2):
            s = at(h, up(near, step), up(far, 2))
            for i in range(2):
                landed(wland.at[h, s, i], w_rs.at[h, s, i])

    for q in range(4):
        for s in range(16):
            wide[s * ROWS : (s + 1) * ROWS] = wland[q // 2, s, q % 2].astype(F32)
        dense[q] = wide[...].astype(BF16)
        if q < 3:
            qkv[q] = dot(normed[...], dense[q], (1, 0)).astype(BF16)
    for m in range(2):
        row = slice(m * 128, (m + 1) * 128)
        for head in range(2):
            col = slice(head * HD, (head + 1) * HD)
            scores = dot(qkv[0, row, col], qkv[1, row, col], (1, 1)) / root
            scores = jnp.exp(scores - jnp.max(scores, axis=-1, keepdims=True))
            prob = scores / jnp.sum(scores, axis=-1, keepdims=True)
            probs[m, head] = prob
            att[row, col] = dot(prob.astype(BF16), qkv[2, row, col], (1, 0)).astype(BF16)

    inc, arrived, parting = (inc_l, inc_r), (arrived_l, arrived_r), (passing_l, passing_r)

    def incoming(m):
        return jnp.concatenate([inc_l[m].reshape(128, LEFT), inc_r[m].reshape(128, D - LEFT)], axis=1).astype(F32)

    def backward(m):
        row = slice(m * 128, (m + 1) * 128)
        scaled_now = (ls_ref[...] * incoming(m)).astype(BF16)
        scaled[row] = scaled_now
        d_att = dot(scaled_now, dense[3], (1, 0)).astype(BF16)
        for head in range(2):
            col = slice(head * HD, (head + 1) * HD)
            d_now = d_att[:, col]
            d_prob = dot(d_now, qkv[2, row, col], (1, 1))
            delta = jnp.sum(d_now.astype(F32) * att[row, col].astype(F32), axis=-1, keepdims=True)
            prob = probs[m, head]
            d_score = (prob * (d_prob - delta) / root).astype(BF16)
            dproj[0, row, col] = dot(d_score, qkv[1, row, col], (1, 0)).astype(BF16)
            dproj[1, row, col] = dot(d_score, qkv[0, row, col], (0, 0)).astype(BF16)
            dproj[2, row, col] = dot(prob.astype(BF16), d_now, (0, 0)).astype(BF16)
        total = dot(dproj[0, row], dense[0], (1, 1))
        total += dot(dproj[1, row], dense[1], (1, 1))
        total += dot(dproj[2, row], dense[2], (1, 1))
        total = total.astype(BF16)
        for other in range(8):
            part[m, other % 2, other // 2] = total[other * 16 : (other + 1) * 16]

    def scale_part(m):
        row = slice(m * 128, (m + 1) * 128)
        out_rows = dot(att[row], dense[3], (1, 1))
        return jnp.sum(incoming(m) * out_rows, axis=0, keepdims=True)

    def remote(src, dst, ss, rs, to):
        return pltpu.make_async_remote_copy(
            src_ref=src, dst_ref=dst, send_sem=ss, recv_sem=rs, device_id=to, device_id_type=MESH
        )

    below = {"tensor": lax.rem(t + 6, 8)}
    section_below = {"pipe": lax.rem(p + 3, 4), "tensor": mirror}

    def first_stage(m):
        return remote(part.at[m, 1 - core], s1land.at[m], c_ss.at[m], c_rs.at[m], {"tensor": partner})

    def across(m, j, c):
        ref = inc[c].at[m, 2 * j + core]
        return remote(ref, ref, a_ss.at[m, c, j], a_rs.at[m, c, 2 * j + core], {"tensor": partner})

    def down(m, j, c):
        ref = inc[c].at[m, 2 * j + core]
        return remote(ref, ref, a_ss.at[m, c, 4 + j], a_rs.at[m, c, 2 * j + core], below)

    def sum_down(m, j, c):
        return remote(parting[c].at[m, j], arrived[c].at[m, j], r_ss.at[m, c, j], r_rs.at[m, c, j], below)

    def hand_on(m, j, c):
        i = 2 * j + core
        return remote(parting[c].at[m, j], inc[c].at[m, i], r_ss.at[m, c, j], a_rs.at[m, c, i], section_below)

    def give_back(m, j):
        return remote(passing.at[m, j], own_out.at[m], o_ss.at[m, j], o_rs.at[m], {"tensor": 2 * j + core})

    def take_piece(m, j):
        for c in range(2):
            landed(inc[c].at[m, 2 * j + core], a_rs.at[m, c, 2 * j + core])

            @pl.when(chip > 0)
            def _():
                down(m, j, c).start()

            across(m, j, c).start()

    def take_rest(m):
        for j in range(4):
            for c in range(2):
                landed(inc[c].at[m, 2 * j + 1 - core], a_rs.at[m, c, 2 * j + 1 - core])

    def reduce_start(m):
        landed(s1land.at[m], c_rs.at[m])

    def reduce_piece(m, j):
        for c, cols in enumerate((slice(0, LEFT), slice(LEFT, D))):
            own = part[m, core, j, :, cols].astype(F32) + s1land[m, j, :, cols].astype(F32)
            running[:, cols] = own

            @pl.when(chip < 3)
            def _():
                landed(arrived[c].at[m, j], r_rs.at[m, c, j])
                running[:, cols] = own + arrived[c][m, j].astype(F32)

            @pl.when(chip > 0)
            def _():
                parting[c][m, j] = running[:, cols].astype(BF16)
                sum_down(m, j, c).start()

        @pl.when(chip == 0)
        def _():
            i = 2 * j + core
            total = running[...]
            rows = xall[i, m].astype(F32)
            inverse = lax.rsqrt(jnp.mean(rows * rows, axis=-1, keepdims=True) + norm_eps)
            unit = rows * inverse
            e = total * gain
            d_input = inverse * (e - unit * jnp.mean(e * unit, axis=-1, keepdims=True))
            held = jnp.concatenate([inc_l[m, i], inc_r[m, i]], axis=1)
            passed = (held.astype(F32) + d_input).astype(BF16)
            passing_l[m, j] = passed[:, :LEFT]
            passing_r[m, j] = passed[:, LEFT:]

            @pl.when(p > 0)
            def _():
                for c in range(2):
                    hand_on(m, j, c).start()

            passing[m, j] = passed
            if j > 0:
                give_back(m, j).start()
            small[1:2] += jnp.sum(total * unit, axis=0, keepdims=True)

    def gcopy(q, kind, second):
        near, far = coords(q // 2)
        ahead, back = (1, 3) if q % 2 == 0 else (3, 1)
        where = back if kind == 1 else ahead
        owner = (2, back, ahead)[kind]
        if second:
            to = at(q // 2, up(near, where), far)
            src, slot, land = gmid_send.at[q, up(near, owner)], 3 + kind, gland2.at[q, kind]
        else:
            to = at(q // 2, near, up(far, where))
            src, slot, land = gsend.at[q, up(far, owner)], kind, gland1.at[q, kind]
        return pltpu.make_async_remote_copy(
            src_ref=src, dst_ref=land, send_sem=g_ss.at[q, slot], recv_sem=g_rs.at[q, slot],
            device_id={"dp": to}, device_id_type=MESH,
        )

    def gsum(q, k):
        near, far = coords(q // 2)
        ahead, back = (1, 3) if q % 2 == 0 else (3, 1)
        place, slot = up(near, (2, back, ahead, 0)[k]), (2, 6, 7, 8)[k]
        return place, pltpu.make_async_remote_copy(
            src_ref=gsend.at[q, up(far, ahead), place], dst_ref=gland1.at[q, 2, place],
            send_sem=g_ss.at[q, slot], recv_sem=g_rs.at[q, slot],
            device_id={"dp": at(q // 2, near, up(far, ahead))}, device_id_type=MESH,
        )

    order = (3, 0, 1, 2)

    def weight_grads():
        for q in order:
            if q == 3:
                wide[...] = dot(scaled[...], att[...], (0, 0))
            else:
                wide[...] = dot(flat[...], dproj[q], (1, 0))
            for s in range(16):
                place = s if q < 2 else (s % SIDE) * SIDE + s // SIDE
                gsend[q, place // SIDE, place % SIDE] = wide[s * ROWS : (s + 1) * ROWS].astype(BF16)
            gcopy(q, 0, False).start()
            gcopy(q, 1, False).start()

    small[...] = jnp.zeros((2, D), F32)

    @pl.when(p == 3)
    def _():
        for m in range(2):
            backward(m)
            first_stage(m).start()
        reduce_start(0)
        for j in range(4):
            reduce_piece(0, j)

    @pl.when(p < 3)
    def _():
        for j in range(4):
            take_piece(0, j)
        take_rest(0)
        backward(0)
        first_stage(0).start()
        reduce_start(0)
        for j in range(4):
            reduce_piece(0, j)
        for j in range(4):
            take_piece(1, j)
        take_rest(1)
        backward(1)
        first_stage(1).start()

        @pl.when(p == 0)
        def _():
            weight_grads()

    reduce_start(1)
    for j in range(4):
        reduce_piece(1, j)

    small[0:1] = scale_part(0) + scale_part(1)
    for k in range(1, 8):
        other = lax.rem(t + k, 8)
        pending.append(send(small, sm_t.at[t], t_ss.at[k], t_rs.at[t], {"tensor": other}))

    @pl.when(p > 0)
    def _():
        weight_grads()

    for q in order:
        near, far = coords(q // 2)
        line = up(far, 1 if q % 2 == 0 else 3)
        landed(gland1.at[q, 0], g_rs.at[q, 0])
        for k in range(4):
            place, copy = gsum(q, k)
            gsend[q, line, place] = (gsend[q, line, place].astype(F32) + gland1[q, 0, place].astype(F32)).astype(BF16)
            copy.start()

    total = small[...]
    for k in range(1, 8):
        other = lax.rem(t + k, 8)
        landed(sm_t.at[other], t_rs.at[other])
        total += sm_t[other]
    sm_send[...] = total
    for k in range(1, 16):
        other = lax.rem(r + k, 16)
        pending.append(send(sm_send, sm_d.at[r], d_ss.at[k], d_rs.at[r], {"dp": other}))

    for k in range(4):
        for q in order:
            near, far = coords(q // 2)
            if k == 0:
                landed(gland1.at[q, 1], g_rs.at[q, 1])
            place, copy = gsum(q, k)
            copy.wait_recv()
            chunk = gsend[q, far, place].astype(F32) + gland1[q, 1, place].astype(F32) + gland1[q, 2, place].astype(F32)
            if k < 2:
                gmid_send[q, place] = chunk.astype(BF16)
                gcopy(q, k, True).start()
            elif k == 2:
                landed(gland2.at[q, 0], g_rs.at[q, 3])
                gmid_send[q, place] = (chunk + gland2[q, 0].astype(F32)).astype(BF16)
                gcopy(q, 2, True).start()
            else:
                gmid[q] = chunk
    stores = []
    for q in order:
        near, far = coords(q // 2)
        landed(gland2.at[q, 1], g_rs.at[q, 4])
        landed(gland2.at[q, 2], g_rs.at[q, 5])
        grad = gmid[q] + gland2[q, 1].astype(F32) + gland2[q, 2].astype(F32)
        for b in (2 * q, 2 * q + 1):
            wload[b] = grad[:, (b % 2) * 128 : (b % 2 + 1) * 128]
            stores.append(pltpu.make_async_copy(wload.at[b], grad_ref.at[:, b], m_s.at[b]))
            stores[-1].start()

    total = sm_send[...]
    for k in range(1, 16):
        other = lax.rem(r + k, 16)
        landed(sm_d.at[other], d_rs.at[other])
        total += sm_d[other]
    sg_ref[...] = total

    for copy in stores:
        copy.wait()
    for copy in pending + x_copies:
        copy.wait_send()
    for q in order:
        for kind in range(3):
            gcopy(q, kind, True).wait_send()
        for kind in range(2):
            gcopy(q, kind, False).wait_send()
        for k in range(4):
            gsum(q, k)[1].wait_send()

    for m in range(2):
        first_stage(m).wait_send()

        @pl.when(p < 3)
        def _():
            for j in range(4):
                for c in range(2):
                    across(m, j, c).wait_send()

            @pl.when(chip > 0)
            def _():
                for j in range(4):
                    for c in range(2):
                        down(m, j, c).wait_send()

        @pl.when(chip > 0)
        def _():
            for j in range(4):
                for c in range(2):
                    sum_down(m, j, c).wait_send()
            landed(own_out.at[m], o_rs.at[m])
            ig_ref[m] = own_out[m]

        @pl.when(chip == 0)
        def _():
            ig_ref[m] = passing[m, 0]
            for j in range(1, 4):
                give_back(m, j).wait_send()

            @pl.when(p > 0)
            def _():
                for j in range(4):
                    for c in range(2):
                        hand_on(m, j, c).wait_send()


def local(x_in, out_grad, layer_scale, norm_gain, master, moment_one, moment_two):
    vmem = pl.BlockSpec(memory_space=pltpu.VMEM)
    dma = pltpu.SemaphoreType.DMA
    scratch = [
        pltpu.VMEM((8, ROWS, 128), F32),
        pltpu.VMEM((2, 16, 2, ROWS, WIDE), BF16),
        pltpu.VMEM((4, D, WIDE), BF16),
        pltpu.VMEM((D, WIDE), F32),
        pltpu.VMEM((8, 2, 16, D), BF16),
        pltpu.VMEM((256, D), BF16),
        pltpu.VMEM((D, 256), BF16),
        pltpu.VMEM((3, 256, WIDE), BF16),
        pltpu.VMEM((2, 2, 128, 128), F32),
        pltpu.VMEM((256, WIDE), BF16),
        pltpu.VMEM((2, 8, 16, LEFT), BF16),
        pltpu.VMEM((2, 8, 16, D - LEFT), BF16),
        pltpu.VMEM((256, D), BF16),
        pltpu.VMEM((3, 256, WIDE), BF16),
        pltpu.VMEM((2, 2, 4, 16, D), BF16),
        pltpu.VMEM((2, 4, 16, D), BF16),
        pltpu.VMEM((2, 4, 16, LEFT), BF16),
        pltpu.VMEM((2, 4, 16, D - LEFT), BF16),
        pltpu.VMEM((2, 4, 16, LEFT), BF16),
        pltpu.VMEM((2, 4, 16, D - LEFT), BF16),
        pltpu.VMEM((2, 4, 16, D), BF16),
        pltpu.VMEM((16, D), F32),
        pltpu.VMEM((2, 16, D), BF16),
        pltpu.VMEM((4, 4, 4, ROWS, WIDE), BF16),
        pltpu.VMEM((4, 3, 4, ROWS, WIDE), BF16),
        pltpu.VMEM((4, ROWS, WIDE), F32),
        pltpu.VMEM((4, 4, ROWS, WIDE), BF16),
        pltpu.VMEM((4, 3, ROWS, WIDE), BF16),
        pltpu.VMEM((2, D), F32),
        pltpu.VMEM((8, 2, D), F32),
        pltpu.VMEM((16, 2, D), F32),
        pltpu.VMEM((2, D), F32),
        dma((8,)),
        dma((2, 20)), dma((2, 16, 2)),
        dma((7,)), dma((8,)),
        dma((2, 2, 8)), dma((2, 2, 8)),
        dma((2,)), dma((2,)),
        dma((2, 2, 4)), dma((2, 2, 4)),
        dma((2, 4)), dma((2,)),
        dma((4, 9)), dma((4, 9)),
        dma((8,)), dma((8,)),
        dma((16,)), dma((16,)),
    ]
    grads, weight_grad, scales = pl.pallas_call(
        kernel,
        out_shape=(
            jax.ShapeDtypeStruct((2, 16, D), BF16),
            jax.ShapeDtypeStruct((ROWS, 8, 128), F32),
            jax.ShapeDtypeStruct((2, D), F32),
        ),
        in_specs=[vmem] * 4 + [pl.BlockSpec(memory_space=pl.ANY)],
        out_specs=(vmem, pl.BlockSpec(memory_space=pl.ANY), vmem),
        scratch_shapes=scratch,
        compiler_params=pltpu.CompilerParams(
            collective_id=0, has_side_effects=True, vmem_limit_bytes=56 * 1024 * 1024
        ),
        cost_estimate=pl.CostEstimate(flops=3 * 10**9, bytes_accessed=10**7, transcendentals=10**5),
    )(
        x_in.reshape(2, 16, D),
        out_grad.reshape(2, 128, D).transpose(0, 2, 1),
        layer_scale,
        norm_gain,
        master.reshape(ROWS, 8, 128),
    )
    bias_one = 1.0 - beta_one**adam_step
    bias_two = 1.0 - beta_two**adam_step
    lines = (ROWS, 8, 128)
    old, one, two = master.reshape(lines), moment_one.reshape(lines), moment_two.reshape(lines)
    old, one, two, weight_grad = lax.optimization_barrier((old, one, two, weight_grad))
    first = beta_one * one + (1.0 - beta_one) * weight_grad
    second = beta_two * two + (1.0 - beta_two) * weight_grad * weight_grad
    update = first / bias_one / (jnp.sqrt(second / bias_two) + adam_eps)
    new_master = old - learn_rate * (update + weight_decay * old)
    shape = master.shape
    return (
        grads.reshape(1, 2, 1, 16, D),
        new_master.reshape(shape),
        first.reshape(shape),
        second.reshape(shape),
        scales[None],
    )


def solution(mesh):
    placed = (
        P("pipe", None, "dp", "tensor", None),
        P(None, "dp", None, None),
        P("pipe", None),
        P("pipe", None),
        P("pipe", "dp", "tensor"),
        P("pipe", "dp", "tensor"),
        P("pipe", "dp", "tensor"),
    )
    return jax.shard_map(
        local,
        mesh=mesh,
        in_specs=placed,
        out_specs=(
            P("pipe", None, "dp", "tensor", None),
            P("pipe", "dp", "tensor"),
            P("pipe", "dp", "tensor"),
            P("pipe", "dp", "tensor"),
            P("pipe", None, None),
        ),
        check_vma=False,
    )
```

```python
import functools
import math

import jax
import jax.numpy as jnp
from jax import lax
from jax.experimental import pallas as pl
from jax.experimental.pallas import tpu as pltpu
from jax.sharding import PartitionSpec as P

HD = 128
LEFT = 896
D = 1600
ROWS = 100
WIDE = 256
SIDE = 4

beta_one = 0.9
beta_two = 0.95
adam_eps = 1e-08
learn_rate = 0.001
weight_decay = 0.05
adam_step = 100.0
norm_eps = 1e-06

F32 = jnp.float32
BF16 = jnp.bfloat16
MESH = pl.DeviceIdType.MESH


def dot(left, right, dims):
    return lax.dot_general(left, right, ((dims[:1], dims[1:]), ((), ())), preferred_element_type=F32)


def kernel(
    x_ref, og_ref, ls_ref, gain_ref, master_ref,
    ig_ref, grad_ref, sg_ref,
    wload, wland, dense, wide, xall, normed, flat, qkv, probs, att, inc_l, inc_r, scaled, dproj,
    part, s1land, arrived_l, arrived_r, passing_l, passing_r, passing, running, own_out, gsend, gland1, gmid, gmid_send, gland2, small, sm_t, sm_d, sm_send,
    m_s, w_ss, w_rs, x_ss, x_rs, a_ss, a_rs, c_ss, c_rs, r_ss, r_rs, o_ss, o_rs, g_ss, g_rs, t_ss, t_rs, d_ss, d_rs,
):
    p = lax.axis_index("pipe")
    r = lax.axis_index("dp")
    t = lax.axis_index("tensor")
    chip = t // 2
    core = t % 2
    y = r // SIDE
    x = r % SIDE
    partner = chip * 2 + (1 - core)
    mirror = (3 - chip) * 2 + core
    root = math.sqrt(HD)

    def up(v, by):
        return lax.rem(v + by, SIDE)

    def send(src, dst, ss, rs, where):
        copy = pltpu.make_async_remote_copy(
            src_ref=src, dst_ref=dst, send_sem=ss, recv_sem=rs, device_id=where, device_id_type=MESH
        )
        copy.start()
        return copy

    def landed(dst, rs):
        pltpu.make_async_remote_copy(
            src_ref=dst, dst_ref=dst, send_sem=rs, recv_sem=rs,
            device_id={"tensor": partner}, device_id_type=MESH,
        ).wait_recv()

    loads = []
    for b in range(8):
        loads.append(pltpu.make_async_copy(master_ref.at[:, b], wload.at[b], m_s.at[b]))
        loads[b].start()

    barrier = pltpu.get_barrier_semaphore()
    for k in range(1, 16):
        pl.semaphore_signal(barrier, inc=1, device_id={"dp": lax.rem(r + k, 16)}, device_id_type=MESH)
    for k in range(1, 8):
        pl.semaphore_signal(barrier, inc=1, device_id={"tensor": lax.rem(t + k, 8)}, device_id_type=MESH)
    for k in (1, 3):
        pl.semaphore_signal(
            barrier, inc=1, device_id={"pipe": lax.rem(p + k, 4), "tensor": mirror}, device_id_type=MESH
        )
    for q in range(4):
        loads[2 * q].wait()
        loads[2 * q + 1].wait()
        wland[q // 2, r, q % 2] = jnp.concatenate([wload[2 * q], wload[2 * q + 1]], axis=1).astype(BF16)
    pl.semaphore_wait(barrier, 24)

    def at(h, near, far):
        return far * SIDE + near if h == 0 else near * SIDE + far

    def coords(h):
        return (x, y) if h == 0 else (y, x)

    def spread(buf, ss, rs):
        copies = [send(buf.at[t], buf.at[t], ss.at[0], rs.at[t], {"tensor": partner})]
        for k in range(1, 4):
            other = up(chip, k) * 2 + core
            copies.append(send(buf.at[t], buf.at[t], ss.at[k], rs.at[t], {"tensor": other}))
        return copies

    def relay(buf, ss, rs):
        copies = []
        for k in range(1, 4):
            other = up(chip, k) * 2 + core
            landed(buf.at[other], rs.at[other])
            copies.append(send(buf.at[other], buf.at[other], ss.at[3 + k], rs.at[other], {"tensor": partner}))
        return copies

    def settle(buf, rs):
        landed(buf.at[partner], rs.at[partner])
        for k in range(1, 4):
            other = up(chip, k) * 2 + 1 - core
            landed(buf.at[other], rs.at[other])

    pending = []

    def wpair(h, s, slot, where):
        pending.append(send(wland.at[h, s], wland.at[h, s], w_ss.at[h, slot], w_rs.at[h, s, 0], {"dp": where}))

    def wone(h, s, i, slot, where):
        pending.append(send(wland.at[h, s, i], wland.at[h, s, i], w_ss.at[h, slot], w_rs.at[h, s, i], {"dp": where}))

    for h in range(2):
        near, far = coords(h)
        wpair(h, r, 0, at(h, up(near, 1), far))
        wpair(h, r, 1, at(h, up(near, 3), far))
    xall[t] = x_ref[...]
    x_copies = spread(xall, x_ss, x_rs)
    for h in range(2):
        near, far = coords(h)
        wpair(h, r, 4, at(h, near, up(far, 1)))
        wpair(h, r, 5, at(h, near, up(far, 3)))
    for h in range(2):
        near, far = coords(h)
        below = at(h, up(near, 3), far)
        above = at(h, up(near, 1), far)
        landed(wland.at[h, below], w_rs.at[h, below, 0])
        wone(h, below, 0, 2, above)
        landed(wland.at[h, above], w_rs.at[h, above, 0])
        wone(h, above, 1, 3, below)
        for j, s in ((1, below), (2, above)):
            wpair(h, s, 4 + 4 * j, at(h, near, up(far, 1)))
            wpair(h, s, 5 + 4 * j, at(h, near, up(far, 3)))
    for h in range(2):
        near, far = coords(h)
        s = at(h, up(near, 2), far)
        for i in range(2):
            landed(wland.at[h, s, i], w_rs.at[h, s, i])
        wpair(h, s, 16, at(h, near, up(far, 1)))
        wpair(h, s, 17, at(h, near, up(far, 3)))

    for j, step in enumerate((0, 3, 1, 2)):
        for h in range(2):
            near, far = coords(h)
            lower = at(h, up(near, step), up(far, 3))
            upper = at(h, up(near, step), up(far, 1))
            landed(wland.at[h, lower], w_rs.at[h, lower, 0])
            wone(h, lower, 0, 6 + 4 * j, at(h, near, up(far, 1)))
            landed(wland.at[h, upper], w_rs.at[h, upper, 0])
            wone(h, upper, 1, 7 + 4 * j, at(h, near, up(far, 3)))
    x_copies += relay(xall, x_ss, x_rs)
    settle(xall, x_rs)

    gain = gain_ref[...]
    for m in range(2):
        rows = xall[:, m].reshape(128, D).astype(F32)
        inverse = lax.rsqrt(jnp.mean(rows * rows, axis=-1, keepdims=True) + norm_eps)
        normed[m * 128 : (m + 1) * 128] = (rows * inverse * gain).astype(BF16)

    @pl.when(p == 3)
    def _():
        for m in range(2):
            rows = og_ref[m].T.reshape(8, 16, D)
            inc_l[m] = rows[:, :, :LEFT]
            inc_r[m] = rows[:, :, LEFT:]

    flat[...] = normed[...].T

    for h in range(2):
        near, far = coords(h)
        for step in (0, 3, 1, 2):
            s = at(h, up(near, step), up(far, 2))
            for i in range(2):
                landed(wland.at[h, s, i], w_rs.at[h, s, i])

    for q in range(4):
        for s in range(16):
            wide[s * ROWS : (s + 1) * ROWS] = wland[q // 2, s, q % 2].astype(F32)
        dense[q] = wide[...].astype(BF16)
        if q < 3:
            qkv[q] = dot(normed[...], dense[q], (1, 0)).astype(BF16)
    for m in range(2):
        row = slice(m * 128, (m + 1) * 128)
        for head in range(2):
            col = slice(head * HD, (head + 1) * HD)
            scores = dot(qkv[0, row, col], qkv[1, row, col], (1, 1)) / root
            scores = jnp.exp(scores - jnp.max(scores, axis=-1, keepdims=True))
            prob = scores / jnp.sum(scores, axis=-1, keepdims=True)
            probs[m, head] = prob
            att[row, col] = dot(prob.astype(BF16), qkv[2, row, col], (1, 0)).astype(BF16)

    inc, arrived, parting = (inc_l, inc_r), (arrived_l, arrived_r), (passing_l, passing_r)

    def incoming(m):
        return jnp.concatenate([inc_l[m].reshape(128, LEFT), inc_r[m].reshape(128, D - LEFT)], axis=1).astype(F32)

    def backward(m):
        row = slice(m * 128, (m + 1) * 128)
        scaled_now = (ls_ref[...] * incoming(m)).astype(BF16)
        scaled[row] = scaled_now
        d_att = dot(scaled_now, dense[3], (1, 0)).astype(BF16)
        for head in range(2):
            col = slice(head * HD, (head + 1) * HD)
            d_now = d_att[:, col]
            d_prob = dot(d_now, qkv[2, row, col], (1, 1))
            delta = jnp.sum(d_now.astype(F32) * att[row, col].astype(F32), axis=-1, keepdims=True)
            prob = probs[m, head]
            d_score = (prob * (d_prob - delta) / root).astype(BF16)
            dproj[0, row, col] = dot(d_score, qkv[1, row, col], (1, 0)).astype(BF16)
            dproj[1, row, col] = dot(d_score, qkv[0, row, col], (0, 0)).astype(BF16)
            dproj[2, row, col] = dot(prob.astype(BF16), d_now, (0, 0)).astype(BF16)
        total = dot(dproj[0, row], dense[0], (1, 1))
        total += dot(dproj[1, row], dense[1], (1, 1))
        total += dot(dproj[2, row], dense[2], (1, 1))
        total = total.astype(BF16)
        for other in range(8):
            part[m, other % 2, other // 2] = total[other * 16 : (other + 1) * 16]

    def scale_part(m):
        row = slice(m * 128, (m + 1) * 128)
        out_rows = dot(att[row], dense[3], (1, 1))
        return jnp.sum(incoming(m) * out_rows, axis=0, keepdims=True)

    def remote(src, dst, ss, rs, to):
        return pltpu.make_async_remote_copy(
            src_ref=src, dst_ref=dst, send_sem=ss, recv_sem=rs, device_id=to, device_id_type=MESH
        )

    below = {"tensor": lax.rem(t + 6, 8)}
    section_below = {"pipe": lax.rem(p + 3, 4), "tensor": mirror}

    def first_stage(m):
        return remote(part.at[m, 1 - core], s1land.at[m], c_ss.at[m], c_rs.at[m], {"tensor": partner})

    def across(m, j, c):
        ref = inc[c].at[m, 2 * j + core]
        return remote(ref, ref, a_ss.at[m, c, j], a_rs.at[m, c, 2 * j + core], {"tensor": partner})

    def down(m, j, c):
        ref = inc[c].at[m, 2 * j + core]
        return remote(ref, ref, a_ss.at[m, c, 4 + j], a_rs.at[m, c, 2 * j + core], below)

    def sum_down(m, j, c):
        return remote(parting[c].at[m, j], arrived[c].at[m, j], r_ss.at[m, c, j], r_rs.at[m, c, j], below)

    def hand_on(m, j, c):
        i = 2 * j + core
        return remote(parting[c].at[m, j], inc[c].at[m, i], r_ss.at[m, c, j], a_rs.at[m, c, i], section_below)

    def give_back(m, j):
        return remote(passing.at[m, j], own_out.at[m], o_ss.at[m, j], o_rs.at[m], {"tensor": 2 * j + core})

    def take_piece(m, j):
        for c in range(2):
            landed(inc[c].at[m, 2 * j + core], a_rs.at[m, c, 2 * j + core])

            @pl.when(chip > 0)
            def _():
                down(m, j, c).start()

            across(m, j, c).start()

    def take_rest(m):
        for j in range(4):
            for c in range(2):
                landed(inc[c].at[m, 2 * j + 1 - core], a_rs.at[m, c, 2 * j + 1 - core])

    def reduce_start(m):
        landed(s1land.at[m], c_rs.at[m])

    def reduce_piece(m, j):
        for c, cols in enumerate((slice(0, LEFT), slice(LEFT, D))):
            own = part[m, core, j, :, cols].astype(F32) + s1land[m, j, :, cols].astype(F32)
            running[:, cols] = own

            @pl.when(chip < 3)
            def _():
                landed(arrived[c].at[m, j], r_rs.at[m, c, j])
                running[:, cols] = own + arrived[c][m, j].astype(F32)

            @pl.when(chip > 0)
            def _():
                parting[c][m, j] = running[:, cols].astype(BF16)
                sum_down(m, j, c).start()

        @pl.when(chip == 0)
        def _():
            i = 2 * j + core
            total = running[...]
            rows = xall[i, m].astype(F32)
            inverse = lax.rsqrt(jnp.mean(rows * rows, axis=-1, keepdims=True) + norm_eps)
            unit = rows * inverse
            e = total * gain
            d_input = inverse * (e - unit * jnp.mean(e * unit, axis=-1, keepdims=True))
            held = jnp.concatenate([inc_l[m, i], inc_r[m, i]], axis=1)
            passed = (held.astype(F32) + d_input).astype(BF16)
            passing_l[m, j] = passed[:, :LEFT]
            passing_r[m, j] = passed[:, LEFT:]

            @pl.when(p > 0)
            def _():
                for c in range(2):
                    hand_on(m, j, c).start()

            passing[m, j] = passed
            if j > 0:
                give_back(m, j).start()
            small[1:2] += jnp.sum(total * unit, axis=0, keepdims=True)

    def gcopy(q, kind, second):
        near, far = coords(q // 2)
        ahead, back = (1, 3) if q % 2 == 0 else (3, 1)
        where = back if kind == 1 else ahead
        owner = (2, back, ahead)[kind]
        if second:
            to = at(q // 2, up(near, where), far)
            src, slot, land = gmid_send.at[q, up(near, owner)], 3 + kind, gland2.at[q, kind]
        else:
            to = at(q // 2, near, up(far, where))
            src, slot, land = gsend.at[q, up(far, owner)], kind, gland1.at[q, kind]
        return pltpu.make_async_remote_copy(
            src_ref=src, dst_ref=land, send_sem=g_ss.at[q, slot], recv_sem=g_rs.at[q, slot],
            device_id={"dp": to}, device_id_type=MESH,
        )

    def gsum(q, k):
        near, far = coords(q // 2)
        ahead, back = (1, 3) if q % 2 == 0 else (3, 1)
        place, slot = up(near, (2, back, ahead, 0)[k]), (2, 6, 7, 8)[k]
        return place, pltpu.make_async_remote_copy(
            src_ref=gsend.at[q, up(far, ahead), place], dst_ref=gland1.at[q, 2, place],
            send_sem=g_ss.at[q, slot], recv_sem=g_rs.at[q, slot],
            device_id={"dp": at(q // 2, near, up(far, ahead))}, device_id_type=MESH,
        )

    order = (3, 0, 1, 2)

    def weight_grads():
        for q in order:
            if q == 3:
                wide[...] = dot(scaled[...], att[...], (0, 0))
            else:
                wide[...] = dot(flat[...], dproj[q], (1, 0))
            for s in range(16):
                place = s if q < 2 else (s % SIDE) * SIDE + s // SIDE
                gsend[q, place // SIDE, place % SIDE] = wide[s * ROWS : (s + 1) * ROWS].astype(BF16)
            gcopy(q, 0, False).start()
            gcopy(q, 1, False).start()

    small[...] = jnp.zeros((2, D), F32)

    @pl.when(p == 3)
    def _():
        for m in range(2):
            backward(m)
            first_stage(m).start()
        reduce_start(0)
        for j in range(4):
            reduce_piece(0, j)

    @pl.when(p < 3)
    def _():
        for j in range(4):
            take_piece(0, j)
        take_rest(0)
        backward(0)
        first_stage(0).start()
        reduce_start(0)
        for j in range(4):
            reduce_piece(0, j)
        for j in range(4):
            take_piece(1, j)
        take_rest(1)
        backward(1)
        first_stage(1).start()

        @pl.when(p == 0)
        def _():
            weight_grads()

    reduce_start(1)
    for j in range(4):
        reduce_piece(1, j)

    @pl.when(p > 0)
    def _():
        weight_grads()

    for q in order:
        near, far = coords(q // 2)
        line = up(far, 1 if q % 2 == 0 else 3)
        landed(gland1.at[q, 0], g_rs.at[q, 0])
        for k in range(4):
            place, copy = gsum(q, k)
            gsend[q, line, place] = (gsend[q, line, place].astype(F32) + gland1[q, 0, place].astype(F32)).astype(BF16)
            copy.start()

    small[0:1] = scale_part(0) + scale_part(1)
    for k in range(1, 8):
        other = lax.rem(t + k, 8)
        pending.append(send(small, sm_t.at[t], t_ss.at[k], t_rs.at[t], {"tensor": other}))

    total = small[...]
    for k in range(1, 8):
        other = lax.rem(t + k, 8)
        landed(sm_t.at[other], t_rs.at[other])
        total += sm_t[other]
    sm_send[...] = total
    for k in range(1, 16):
        other = lax.rem(r + k, 16)
        pending.append(send(sm_send, sm_d.at[r], d_ss.at[k], d_rs.at[r], {"dp": other}))

    for k in range(4):
        for q in order:
            near, far = coords(q // 2)
            if k == 0:
                landed(gland1.at[q, 1], g_rs.at[q, 1])
            place, copy = gsum(q, k)
            copy.wait_recv()
            chunk = gsend[q, far, place].astype(F32) + gland1[q, 1, place].astype(F32) + gland1[q, 2, place].astype(F32)
            if k < 2:
                gmid_send[q, place] = chunk.astype(BF16)
                gcopy(q, k, True).start()
            elif k == 2:
                landed(gland2.at[q, 0], g_rs.at[q, 3])
                gmid_send[q, place] = (chunk + gland2[q, 0].astype(F32)).astype(BF16)
                gcopy(q, 2, True).start()
            else:
                gmid[q] = chunk
    stores = []
    for q in order:
        near, far = coords(q // 2)
        landed(gland2.at[q, 1], g_rs.at[q, 4])
        landed(gland2.at[q, 2], g_rs.at[q, 5])
        grad = gmid[q] + gland2[q, 1].astype(F32) + gland2[q, 2].astype(F32)
        for b in (2 * q, 2 * q + 1):
            wload[b] = grad[:, (b % 2) * 128 : (b % 2 + 1) * 128]
            stores.append(pltpu.make_async_copy(wload.at[b], grad_ref.at[:, b], m_s.at[b]))
            stores[-1].start()

    total = sm_send[...]
    for k in range(1, 16):
        other = lax.rem(r + k, 16)
        landed(sm_d.at[other], d_rs.at[other])
        total += sm_d[other]
    sg_ref[...] = total

    for copy in stores:
        copy.wait()
    for copy in pending + x_copies:
        copy.wait_send()
    for q in order:
        for kind in range(3):
            gcopy(q, kind, True).wait_send()
        for kind in range(2):
            gcopy(q, kind, False).wait_send()
        for k in range(4):
            gsum(q, k)[1].wait_send()

    for m in range(2):
        first_stage(m).wait_send()

        @pl.when(p < 3)
        def _():
            for j in range(4):
                for c in range(2):
                    across(m, j, c).wait_send()

            @pl.when(chip > 0)
            def _():
                for j in range(4):
                    for c in range(2):
                        down(m, j, c).wait_send()

        @pl.when(chip > 0)
        def _():
            for j in range(4):
                for c in range(2):
                    sum_down(m, j, c).wait_send()
            landed(own_out.at[m], o_rs.at[m])
            ig_ref[m] = own_out[m]

        @pl.when(chip == 0)
        def _():
            ig_ref[m] = passing[m, 0]
            for j in range(1, 4):
                give_back(m, j).wait_send()

            @pl.when(p > 0)
            def _():
                for j in range(4):
                    for c in range(2):
                        hand_on(m, j, c).wait_send()


def local(x_in, out_grad, layer_scale, norm_gain, master, moment_one, moment_two):
    vmem = pl.BlockSpec(memory_space=pltpu.VMEM)
    dma = pltpu.SemaphoreType.DMA
    scratch = [
        pltpu.VMEM((8, ROWS, 128), F32),
        pltpu.VMEM((2, 16, 2, ROWS, WIDE), BF16),
        pltpu.VMEM((4, D, WIDE), BF16),
        pltpu.VMEM((D, WIDE), F32),
        pltpu.VMEM((8, 2, 16, D), BF16),
        pltpu.VMEM((256, D), BF16),
        pltpu.VMEM((D, 256), BF16),
        pltpu.VMEM((3, 256, WIDE), BF16),
        pltpu.VMEM((2, 2, 128, 128), F32),
        pltpu.VMEM((256, WIDE), BF16),
        pltpu.VMEM((2, 8, 16, LEFT), BF16),
        pltpu.VMEM((2, 8, 16, D - LEFT), BF16),
        pltpu.VMEM((256, D), BF16),
        pltpu.VMEM((3, 256, WIDE), BF16),
        pltpu.VMEM((2, 2, 4, 16, D), BF16),
        pltpu.VMEM((2, 4, 16, D), BF16),
        pltpu.VMEM((2, 4, 16, LEFT), BF16),
        pltpu.VMEM((2, 4, 16, D - LEFT), BF16),
        pltpu.VMEM((2, 4, 16, LEFT), BF16),
        pltpu.VMEM((2, 4, 16, D - LEFT), BF16),
        pltpu.VMEM((2, 4, 16, D), BF16),
        pltpu.VMEM((16, D), F32),
        pltpu.VMEM((2, 16, D), BF16),
        pltpu.VMEM((4, 4, 4, ROWS, WIDE), BF16),
        pltpu.VMEM((4, 3, 4, ROWS, WIDE), BF16),
        pltpu.VMEM((4, ROWS, WIDE), F32),
        pltpu.VMEM((4, 4, ROWS, WIDE), BF16),
        pltpu.VMEM((4, 3, ROWS, WIDE), BF16),
        pltpu.VMEM((2, D), F32),
        pltpu.VMEM((8, 2, D), F32),
        pltpu.VMEM((16, 2, D), F32),
        pltpu.VMEM((2, D), F32),
        dma((8,)),
        dma((2, 20)), dma((2, 16, 2)),
        dma((7,)), dma((8,)),
        dma((2, 2, 8)), dma((2, 2, 8)),
        dma((2,)), dma((2,)),
        dma((2, 2, 4)), dma((2, 2, 4)),
        dma((2, 4)), dma((2,)),
        dma((4, 9)), dma((4, 9)),
        dma((8,)), dma((8,)),
        dma((16,)), dma((16,)),
    ]
    grads, weight_grad, scales = pl.pallas_call(
        kernel,
        out_shape=(
            jax.ShapeDtypeStruct((2, 16, D), BF16),
            jax.ShapeDtypeStruct((ROWS, 8, 128), F32),
            jax.ShapeDtypeStruct((2, D), F32),
        ),
        in_specs=[vmem] * 4 + [pl.BlockSpec(memory_space=pl.ANY)],
        out_specs=(vmem, pl.BlockSpec(memory_space=pl.ANY), vmem),
        scratch_shapes=scratch,
        compiler_params=pltpu.CompilerParams(
            collective_id=0, has_side_effects=True, vmem_limit_bytes=56 * 1024 * 1024
        ),
        cost_estimate=pl.CostEstimate(flops=3 * 10**9, bytes_accessed=10**7, transcendentals=10**5),
    )(
        x_in.reshape(2, 16, D),
        out_grad.reshape(2, 128, D).transpose(0, 2, 1),
        layer_scale,
        norm_gain,
        master.reshape(ROWS, 8, 128),
    )
    bias_one = 1.0 - beta_one**adam_step
    bias_two = 1.0 - beta_two**adam_step
    lines = (ROWS, 8, 128)
    old, one, two = master.reshape(lines), moment_one.reshape(lines), moment_two.reshape(lines)
    old, one, two, weight_grad = lax.optimization_barrier((old, one, two, weight_grad))
    first = beta_one * one + (1.0 - beta_one) * weight_grad
    second = beta_two * two + (1.0 - beta_two) * weight_grad * weight_grad
    update = first / bias_one / (jnp.sqrt(second / bias_two) + adam_eps)
    new_master = old - learn_rate * (update + weight_decay * old)
    shape = master.shape
    return (
        grads.reshape(1, 2, 1, 16, D),
        new_master.reshape(shape),
        first.reshape(shape),
        second.reshape(shape),
        scales[None],
    )


def solution(mesh):
    placed = (
        P("pipe", None, "dp", "tensor", None),
        P(None, "dp", None, None),
        P("pipe", None),
        P("pipe", None),
        P("pipe", "dp", "tensor"),
        P("pipe", "dp", "tensor"),
        P("pipe", "dp", "tensor"),
    )
    return jax.shard_map(
        local,
        mesh=mesh,
        in_specs=placed,
        out_specs=(
            P("pipe", None, "dp", "tensor", None),
            P("pipe", "dp", "tensor"),
            P("pipe", "dp", "tensor"),
            P("pipe", "dp", "tensor"),
            P("pipe", None, None),
        ),
        check_vma=False,
    )
```
